32 devices in a mesh: space: 16 (over z, y, x), feat: 2 (over core).
Axes of the slice: x: 2, y: 2, z: 4, core: 2. Of those that a mesh axis runs over, the one named last changes fastest.
Arguments:
- nodes: bfloat16 [2560, 512], P('space'), may hold values from -6 to 6
- edges: bfloat16 [12288, 512], P(('space', 'feat')), may hold values from -6 to 6
- senders: int32 [12288], P(('space', 'feat')), may hold values from 0 to 2559, as said below
- receivers: int32 [12288], P(('space', 'feat')), may hold values from 0 to 2559, as said below
- edge_proj: bfloat16 [512, 512], replicated, may hold values from -0.15625 to 0.15625
- send_proj: bfloat16 [512, 512], replicated, may hold values from -0.15625 to 0.15625
- recv_proj: bfloat16 [512, 512], replicated, may hold values from -0.15625 to 0.15625
- edge_bias: float32 [512], replicated, may hold values from -3 to 3
- edge_out: bfloat16 [512, 512], replicated, may hold values from -0.25 to 0.25
- edge_gain: float32 [512], replicated, may hold values from 0.25 to 1.75
- edge_shift: float32 [512], replicated, may hold values from -3 to 3
- node_in: bfloat16 [1024, 512], replicated, may hold values from -0.1875 to 0.1875
- node_bias: float32 [512], replicated, may hold values from -3 to 3
- node_out: bfloat16 [512, 512], replicated, may hold values from -0.25 to 0.25
- node_gain: float32 [512], replicated, may hold values from 0.25 to 1.75
- node_shift: float32 [512], replicated, may hold values from -3 to 3
- node_cot: bfloat16 [2560, 512], P('space'), may hold values from -6 to 6
Outputs:
- new_nodes: bfloat16 [2560, 512], P('space')
- node_grad: bfloat16 [2560, 512], P('space')
- edge_grad: bfloat16 [12288, 512], P(('space', 'feat'))
The draws below stay inside these ranges and needn't reach their ends.
Inputs may be any that keep to these rules, and one draw needn't show every extreme that they name: `senders`: every edge of a block's 768 has its receiver in that block; its sender lies in the same block, in the last 48 rows of the previous block, in the first 48 rows of the next block, or among the first 2 rows of any block. `receivers`: every edge of a block's 768 has its receiver among that block's 160 nodes.
All inputs are finite; a program needn't handle non-finite values.
Results may differ from the reference program's by a relative error of at most 0.0077.
Values may be sent and summed in bfloat16 or wider, within the bound.
A program may use at most 64 MiB of HBM per device.

```python
import jax
import jax.numpy as jnp
from jax import lax

D = 512
NODE_DEV = 160
EDGE_DEV = 768
RIM = 48
HUB_DEV = 2
NODES = 2560
EDGES = 12288


def draw_senders(key, part):
    blocks = NODES // NODE_DEV
    subkeys = jax.random.split(key, 5)
    position = jnp.arange(EDGES, dtype=jnp.int32)
    owner_block = position // EDGE_DEV
    category = jax.random.randint(subkeys[0], (EDGES,), 0, 5)
    own_row = jax.random.randint(subkeys[1], (EDGES,), 0, NODE_DEV)
    rim_row = jax.random.randint(subkeys[2], (EDGES,), 0, RIM)
    hub_block = jax.random.randint(subkeys[3], (EDGES,), 0, blocks)
    hub_row = jax.random.randint(subkeys[4], (EDGES,), 0, HUB_DEV)
    own_id = owner_block * NODE_DEV + own_row
    left_id = jnp.where(owner_block > 0, (owner_block - 1) * NODE_DEV + NODE_DEV - RIM + rim_row, own_id)
    right_id = jnp.where(owner_block < blocks - 1, (owner_block + 1) * NODE_DEV + rim_row, own_id)
    hub_id = hub_block * NODE_DEV + hub_row
    chosen = jnp.where(category == 2, left_id, jnp.where(category == 3, right_id, jnp.where(category == 4, hub_id, own_id)))
    chosen = jnp.where(position == 0, 0, chosen)
    chosen = jnp.where(position == EDGES - 1, NODES - 1, chosen)
    return chosen.astype(jnp.int32)


def draw_receivers(key, part):
    folded = jax.random.fold_in(key, 7)
    position = jnp.arange(EDGES, dtype=jnp.int32)
    owner_block = position // EDGE_DEV
    own_row = jax.random.randint(folded, (EDGES,), 0, NODE_DEV)
    own_row = jnp.where(position == 0, 0, own_row)
    own_row = jnp.where(position == EDGES - 1, NODE_DEV - 1, own_row)
    return (owner_block * NODE_DEV + own_row).astype(jnp.int32)


def levels(key, shape, shards, smallest, high):
    level, own = 1.0, jax.random.fold_in(key, 6)
    for dim, shards_of in shards:
        draws = jnp.exp(jax.random.uniform(jax.random.fold_in(own, dim), (shards_of,), jnp.float32, smallest / len(shards), high / len(shards)))
        level = level * jnp.repeat(draws, shape[dim] // shards_of).reshape([-1 if axis == dim else 1 for axis in range(len(shape))])
    return level


def bell_draw(rng, dims, scale, reach, shards=(), kind=jnp.bfloat16):
    values = scale * jax.random.normal(rng, dims, jnp.float32)
    if shards:
        values = values * levels(rng, dims, shards, -0.22, 0.18)
    return jnp.clip(values, -reach, reach).astype(kind)


def setup_inputs(seed: int = 0) -> dict:
    keys = jax.random.split(jax.random.key(seed), 18)
    return {
        "nodes": bell_draw(keys[0], (NODES, D), 1.0, 6.0, ((0, 16),)),
        "edges": bell_draw(keys[1], (EDGES, D), 1.0, 6.0, ((0, 32),)),
        "senders": draw_senders(jax.random.fold_in(keys[17], 71), 0),
        "receivers": draw_receivers(jax.random.fold_in(keys[17], 71), 0),
        "edge_proj": bell_draw(keys[4], (D, D), (3 * D) ** -0.5, 0.15625),
        "send_proj": bell_draw(keys[5], (D, D), (3 * D) ** -0.5, 0.15625),
        "recv_proj": bell_draw(keys[6], (D, D), (3 * D) ** -0.5, 0.15625),
        "edge_bias": bell_draw(keys[7], (D,), 0.5, 3.0, (), jnp.float32),
        "edge_out": bell_draw(keys[8], (D, D), D ** -0.5, 0.25),
        "edge_gain": jnp.clip(1.0 + 0.15 * jax.random.normal(keys[9], (D,), jnp.float32), 0.25, 1.75),
        "edge_shift": bell_draw(keys[10], (D,), 0.5, 3.0, (), jnp.float32),
        "node_in": bell_draw(keys[11], (2 * D, D), (2 * D) ** -0.5, 0.1875),
        "node_bias": bell_draw(keys[12], (D,), 0.5, 3.0, (), jnp.float32),
        "node_out": bell_draw(keys[13], (D, D), D ** -0.5, 0.25),
        "node_gain": jnp.clip(1.0 + 0.15 * jax.random.normal(keys[14], (D,), jnp.float32), 0.25, 1.75),
        "node_shift": bell_draw(keys[15], (D,), 0.5, 3.0, (), jnp.float32),
        "node_cot": bell_draw(keys[16], (NODES, D), 1.0, 6.0, ((0, 16),)),
    }


epsilon = 1e-05

def layer_stats(values):
    average = lax.optimization_barrier(jnp.mean(values, axis=-1, keepdims=True))
    centred = values - average
    inv_scale = lax.rsqrt(lax.optimization_barrier(jnp.mean(centred * centred, axis=-1, keepdims=True)) + epsilon)
    return (centred * inv_scale, inv_scale)

def norm_back(upstream, normed, inv_scale, gain_vec):
    scaled = upstream * gain_vec
    return inv_scale * (scaled - lax.optimization_barrier(jnp.mean(scaled, axis=-1, keepdims=True)) - normed * lax.optimization_barrier(jnp.mean(scaled * normed, axis=-1, keepdims=True)))

def swish_slope(preact):
    sigmoid_val = jax.nn.sigmoid(preact)
    return sigmoid_val * (1.0 + preact * (1.0 - sigmoid_val))

def reference(nodes, edges, senders, receivers, edge_proj, send_proj, recv_proj, edge_bias, edge_out, edge_gain, edge_shift, node_in, node_bias, node_out, node_gain, node_shift, node_cot):
    width = nodes.shape[1]
    node_total = nodes.shape[0]
    send_terms = jnp.dot(nodes, send_proj, preferred_element_type=jnp.float32).astype(jnp.bfloat16)
    recv_terms = jnp.dot(nodes, recv_proj, preferred_element_type=jnp.float32).astype(jnp.bfloat16)
    hidden_pre = jnp.dot(edges, edge_proj, preferred_element_type=jnp.float32) + jnp.take(send_terms, senders, axis=0).astype(jnp.float32) + jnp.take(recv_terms, receivers, axis=0).astype(jnp.float32) + edge_bias
    hidden_act = jax.nn.silu(hidden_pre).astype(jnp.bfloat16)
    edge_sum = jnp.dot(hidden_act, edge_out, preferred_element_type=jnp.float32)
    edge_normed, edge_scale = layer_stats(edge_sum)
    new_edges = (edges.astype(jnp.float32) + edge_normed * edge_gain + edge_shift).astype(jnp.bfloat16)
    gathered = jax.ops.segment_sum(new_edges.astype(jnp.float32), receivers, num_segments=node_total).astype(jnp.bfloat16)
    node_pre = jnp.dot(nodes, node_in[:width], preferred_element_type=jnp.float32) + jnp.dot(gathered, node_in[width:], preferred_element_type=jnp.float32) + node_bias
    node_act = jax.nn.silu(node_pre).astype(jnp.bfloat16)
    node_mix = jnp.dot(node_act, node_out, preferred_element_type=jnp.float32)
    node_normed, node_scale = layer_stats(node_mix)
    new_nodes = (nodes.astype(jnp.float32) + node_normed * node_gain + node_shift).astype(jnp.bfloat16)
    upstream = node_cot.astype(jnp.float32)
    node_dmix = norm_back(upstream, node_normed, node_scale, node_gain).astype(jnp.bfloat16)
    node_dact = jnp.dot(node_dmix, node_out.T, preferred_element_type=jnp.float32)
    node_dpre = (node_dact * swish_slope(node_pre)).astype(jnp.bfloat16)
    node_direct = upstream + jnp.dot(node_dpre, node_in[:width].T, preferred_element_type=jnp.float32)
    gathered_grad = jnp.dot(node_dpre, node_in[width:].T, preferred_element_type=jnp.float32)
    edge_upstream = jnp.take(gathered_grad, receivers, axis=0)
    edge_dsum = norm_back(edge_upstream, edge_normed, edge_scale, edge_gain).astype(jnp.bfloat16)
    edge_dact = jnp.dot(edge_dsum, edge_out.T, preferred_element_type=jnp.float32)
    edge_dpre = (edge_dact * swish_slope(hidden_pre)).astype(jnp.bfloat16)
    edge_grad = (edge_upstream + jnp.dot(edge_dpre, edge_proj.T, preferred_element_type=jnp.float32)).astype(jnp.bfloat16)
    send_sums = jax.ops.segment_sum(edge_dpre.astype(jnp.float32), senders, num_segments=node_total)
    recv_sums = jax.ops.segment_sum(edge_dpre.astype(jnp.float32), receivers, num_segments=node_total)
    send_part = jnp.dot(send_sums, send_proj.astype(jnp.float32).T, precision=lax.Precision.HIGHEST)
    recv_part = jnp.dot(recv_sums, recv_proj.astype(jnp.float32).T, precision=lax.Precision.HIGHEST)
    node_grad = (node_direct + send_part + recv_part).astype(jnp.bfloat16)
    return (new_nodes, node_grad, edge_grad)
```

```python
import functools

import jax
import jax.numpy as jnp
from jax import lax
from jax.experimental import pallas as pl
from jax.experimental.pallas import tpu as pltpu
from jax.sharding import PartitionSpec as P

RIM = 48
HUB_DEV = 2
LANES = 128
CHUNK = 64
epsilon = 1e-05

F32 = jnp.float32
BF16 = jnp.bfloat16
MESH = pl.DeviceIdType.MESH


def mm(a, b):
    return jnp.dot(a, b, preferred_element_type=F32)


def mm_t(a, b):
    return lax.dot_general(a, b, (((1,), (1,)), ((), ())), preferred_element_type=F32)


def sigmoid(v):
    return 0.5 * jnp.tanh(0.5 * v) + 0.5


def mean_row(v):
    return jnp.mean(v, axis=-1, keepdims=True)


def late_ids(index, own_block, blocks, rows):
    left = (own_block * rows - RIM) + index
    right = (own_block + 1) * rows + (index - RIM)
    hub = index - 2 * RIM
    row = jnp.zeros_like(hub)
    for step in range(1, HUB_DEV):
        row = row + jnp.where(hub >= step * blocks, 1, 0)
    block = hub - row * blocks
    hub_id = block * rows + row
    hub_id = jnp.where((block == own_block) | (block == own_block + 1), -1, hub_id)
    return jnp.where(index < RIM, left, jnp.where(index < 2 * RIM, right, hub_id))


def onehot(a, b):
    return jnp.where(a == b, 1.0, 0.0).astype(BF16)


def kernel(
    blocks,
    send_id, recv_id, nodes, edges, w_edge, w_send, w_recv, bias, w_out, gain_e, shift_e,
    w_in, bias_n, w_mix, gain_n, shift_n, cot,
    out_nodes, out_grad, out_edges,
    v_send_id, v_recv_id, v_nodes, v_edges, v_edge, v_send, v_recv, v_bias, v_out, v_gain_e, v_shift_e,
    v_in, v_bias_n, v_mix, v_gain_n, v_shift_n, v_cot,
    v_late, v_hub_src, v_hub, oh_own, oh_recv, oh_late,
    v_hidden, v_slope, v_act, v_normed, v_scale, v_new,
    g_mine, g_peer, v_pre, v_dpre, v_direct, v_up, v_dsum, v_edpre,
    rim_out, rim_back, hub_out, hub_back, p_mine, p_peer, x_mine, x_peer,
    o_nodes, o_grad, o_edges,
    load_sem, store_sem, rim_send, rim_recv, hub_send, hub_recv, peer_send, peer_recv,
):
    me = lax.axis_index("space")
    core = lax.axis_index("feat")
    rows, width = v_nodes.shape
    count = v_edges.shape[0]
    pieces = width // LANES
    tile = HUB_DEV * pieces
    peer = (me, 1 - core)
    left, right = (me - 1, core), (me + 1, core)
    has_left, has_right = me > 0, me < blocks - 1

    barrier = pltpu.get_barrier_semaphore()

    def greet(step, carry):
        other = lax.rem(me + step, blocks)
        pl.semaphore_signal(barrier, inc=1, device_id=(other, core), device_id_type=MESH)
        return carry

    lax.fori_loop(1, blocks, greet, 0)
    pl.semaphore_signal(barrier, inc=1, device_id=peer, device_id_type=MESH)

    pairs = [
        (nodes, v_nodes), (send_id, v_send_id), (recv_id, v_recv_id), (w_recv, v_recv), (w_send, v_send),
        (edges, v_edges), (w_edge, v_edge), (bias, v_bias), (w_out, v_out), (gain_e, v_gain_e), (shift_e, v_shift_e),
        (w_in, v_in), (bias_n, v_bias_n), (w_mix, v_mix), (gain_n, v_gain_n), (shift_n, v_shift_n), (cot, v_cot),
    ]
    loads = [pltpu.make_async_copy(src, dst, load_sem.at[k]) for k, (src, dst) in enumerate(pairs)]
    for load in loads:
        load.start()

    def ready(*refs):
        for k, (_, dst) in enumerate(pairs):
            if any(dst is ref for ref in refs):
                loads[k].wait()

    def remote(src, dst, send_sem, recv_sem, device):
        return pltpu.make_async_remote_copy(
            src_ref=src, dst_ref=dst, send_sem=send_sem, recv_sem=recv_sem, device_id=device, device_id_type=MESH
        )

    my_slot = pl.ds(pl.multiple_of(me * tile, tile), tile)

    def hub_copy(step, src, dst, kind):
        other = lax.rem(me + step, blocks)
        return remote(src(other), dst.at[my_slot], hub_send.at[kind], hub_recv.at[kind], (other, core))

    def hub_wait(buffer, sem):
        part = buffer.at[pl.ds(0, (blocks - 1) * tile)]
        pltpu.make_async_copy(part, part, sem).wait()

    ready(v_nodes)
    head = v_nodes[0:16, :].astype(F32)
    for j in range(pieces):
        v_hub_src[HUB_DEV * j : HUB_DEV * (j + 1), :] = head[0:HUB_DEV, LANES * j : LANES * (j + 1)]
    v_hub[my_slot, :] = v_hub_src[...]
    hub_back[my_slot, :] = jnp.zeros((tile, LANES), F32)
    zero_rim = jnp.zeros((RIM, width), BF16)

    @pl.when(jnp.logical_not(has_left))
    def _():
        v_late[0:RIM, :] = zero_rim
        rim_back[0:RIM, :] = zero_rim

    @pl.when(jnp.logical_not(has_right))
    def _():
        v_late[RIM : 2 * RIM, :] = zero_rim
        rim_back[RIM : 2 * RIM, :] = zero_rim

    pl.semaphore_wait(barrier, blocks)

    low, high = pl.ds(0, RIM), pl.ds(RIM, RIM)
    to_right = remote(nodes.at[pl.ds(rows - RIM, RIM)], v_late.at[low], rim_send.at[0], rim_recv.at[0], right)
    to_left = remote(nodes.at[pl.ds(0, RIM)], v_late.at[high], rim_send.at[1], rim_recv.at[1], left)

    @pl.when(has_right)
    def _():
        to_right.start()

    @pl.when(has_left)
    def _():
        to_left.start()

    def push_hub(step, carry):
        hub_copy(step, lambda other: v_hub_src, v_hub, 0).start()
        return carry

    lax.fori_loop(1, blocks, push_hub, 0)

    ready(v_send_id, v_recv_id)
    ids_s, ids_r = v_send_id[...], v_recv_id[...]
    col_s = jnp.transpose(jnp.broadcast_to(ids_s, (LANES, count)))[:, 0:1]
    col_r = jnp.transpose(jnp.broadcast_to(ids_r, (LANES, count)))[:, 0:1]
    own_ids = lax.broadcasted_iota(jnp.int32, (1, rows), 1) + me * rows
    late_count = v_late.shape[0]
    late_row = late_ids(lax.broadcasted_iota(jnp.int32, (1, late_count), 1), me, blocks, rows)
    oh_own[...] = onehot(col_s, own_ids)
    oh_recv[...] = onehot(col_r, own_ids)
    oh_late[...] = onehot(col_s, late_row)

    ready(v_recv, v_send)
    recv_terms = mm(v_nodes[...], v_recv[...]).astype(BF16)
    send_terms = mm(v_nodes[...], v_send[...]).astype(BF16)
    ready(v_edges, v_edge, v_bias)
    v_hidden[...] = (
        mm(v_edges[...], v_edge[...]) + mm(oh_recv[...], recv_terms) + mm(oh_own[...], send_terms) + v_bias[...]
    )

    @pl.when(has_left)
    def _():
        to_right.wait_recv()

    @pl.when(has_right)
    def _():
        to_left.wait_recv()

    hub_wait(v_hub, hub_recv.at[0])
    for r in range(HUB_DEV):
        for j in range(pieces):
            part = v_hub[pl.ds(HUB_DEV * j + r, blocks, stride=tile), :]
            v_late[2 * RIM + r * blocks : 2 * RIM + (r + 1) * blocks, LANES * j : LANES * (j + 1)] = part.astype(BF16)
    late_terms = mm(v_late[...], v_send[...]).astype(BF16)
    v_hidden[...] += mm(oh_late[...], late_terms)

    chunks = [pl.ds(start, CHUNK) for start in range(0, count, CHUNK)]
    for at in chunks:
        pre = v_hidden[at, :]
        sig = sigmoid(pre)
        act = pre * sig
        v_act[at, :] = act.astype(BF16)
        v_slope[at, :] = sig + act * (1.0 - sig)
    ready(v_out, v_gain_e, v_shift_e)
    v_hidden[...] = mm(v_act[...], v_out[...])
    for at in chunks:
        total = v_hidden[at, :]
        centred = total - mean_row(total)
        inv = lax.rsqrt(mean_row(centred * centred) + epsilon)
        normed = centred * inv
        v_normed[at, :] = normed
        v_scale[at, :] = jnp.broadcast_to(inv, (CHUNK, LANES))
        v_new[at, :] = (v_edges[at, :].astype(F32) + normed * v_gain_e[...] + v_shift_e[...]).astype(BF16)

    own_col = lax.broadcasted_iota(jnp.int32, (rows, 1), 0) + me * rows
    t_recv = onehot(own_col, ids_r)
    g_mine[...] = mm(t_recv, v_new[...]).astype(BF16)
    gather_copy = remote(g_mine, g_peer, peer_send.at[0], peer_recv.at[0], peer)
    gather_copy.start()

    ready(v_in, v_bias_n, v_mix, v_gain_n, v_shift_n, v_cot)
    v_pre[...] = mm(v_nodes[...], v_in[0:width, :]) + v_bias_n[...]
    gather_copy.wait_recv()
    gathered = (g_mine[...].astype(F32) + g_peer[...].astype(F32)).astype(BF16)
    pre = v_pre[...] + mm(gathered, v_in[width : 2 * width, :])
    sig = sigmoid(pre)
    act = pre * sig
    v_pre[...] = sig + act * (1.0 - sig)
    mix = mm(act.astype(BF16), v_mix[...])
    centred = mix - mean_row(mix)
    inv = lax.rsqrt(mean_row(centred * centred) + epsilon)
    normed = centred * inv
    o_nodes[...] = (v_nodes[...].astype(F32) + normed * v_gain_n[...] + v_shift_n[...]).astype(BF16)
    store_nodes = pltpu.make_async_copy(o_nodes, out_nodes, store_sem.at[0])
    store_nodes.start()
    scaled = v_cot[...].astype(F32) * v_gain_n[...]
    dmix = (inv * (scaled - mean_row(scaled) - normed * mean_row(scaled * normed))).astype(BF16)
    v_dpre[...] = (mm_t(dmix, v_mix[...]) * v_pre[...]).astype(BF16)
    gathered_grad = mm_t(v_dpre[...], v_in[width : 2 * width, :]).astype(BF16)

    v_up[...] = mm(oh_recv[...], gathered_grad)
    for at in chunks:
        normed = v_normed[at, :]
        scaled = v_up[at, :] * v_gain_e[...]
        v_dsum[at, :] = (
            v_scale[at, 0:1] * (scaled - mean_row(scaled) - normed * mean_row(scaled * normed))
        ).astype(BF16)
    v_hidden[...] = mm_t(v_dsum[...], v_out[...])
    for at in chunks:
        v_edpre[at, :] = (v_hidden[at, :] * v_slope[at, :]).astype(BF16)

    late_col = late_ids(lax.broadcasted_iota(jnp.int32, (late_count, 1), 0), me, blocks, rows)
    t_late = onehot(late_col, ids_s)
    late_sums = mm(t_late, v_edpre[...]).astype(BF16)
    late_part = mm_t(late_sums, v_send[...])
    rim_out[...] = late_part[0 : 2 * RIM, :].astype(BF16)
    back_left = remote(rim_out.at[low], rim_back.at[high], rim_send.at[2], rim_recv.at[2], left)
    back_right = remote(rim_out.at[high], rim_back.at[low], rim_send.at[3], rim_recv.at[3], right)

    @pl.when(has_left)
    def _():
        back_left.start()

    @pl.when(has_right)
    def _():
        back_right.start()

    for r in range(HUB_DEV):
        for j in range(pieces):
            hub_out[pl.ds(HUB_DEV * j + r, blocks, stride=tile), :] = late_part[
                2 * RIM + r * blocks : 2 * RIM + (r + 1) * blocks, LANES * j : LANES * (j + 1)
            ]

    def hub_part(other):
        return hub_out.at[pl.ds(pl.multiple_of(other * tile, tile), tile)]

    def return_hub(step, carry):
        hub_copy(step, hub_part, hub_back, 1).start()
        return carry

    lax.fori_loop(1, blocks, return_hub, 0)

    t_own = onehot(own_col, ids_s)
    t_recv = onehot(own_col, ids_r)
    send_sums = mm(t_own, v_edpre[...]).astype(BF16)
    recv_sums = mm(t_recv, v_edpre[...]).astype(BF16)
    p_mine[...] = (mm_t(send_sums, v_send[...]) + mm_t(recv_sums, v_recv[...])).astype(BF16)
    part_copy = remote(p_mine, p_peer, peer_send.at[1], peer_recv.at[1], peer)
    part_copy.start()

    o_edges[...] = (v_up[...] + mm_t(v_edpre[...], v_edge[...])).astype(BF16)
    store_edges = pltpu.make_async_copy(o_edges, out_edges, store_sem.at[1])
    store_edges.start()
    v_direct[...] = v_cot[...].astype(F32) + mm_t(v_dpre[...], v_in[0:width, :])

    @pl.when(has_right)
    def _():
        back_left.wait_recv()

    @pl.when(has_left)
    def _():
        back_right.wait_recv()

    hub_wait(hub_back, hub_recv.at[1])
    hub_sum = jnp.sum(hub_back[...].reshape(blocks, tile, LANES), axis=0)
    v_up[0:tile, 0:LANES] = hub_sum
    v_hidden[0:16, :] = jnp.zeros((16, width), F32)
    for j in range(pieces):
        v_hidden[0:HUB_DEV, LANES * j : LANES * (j + 1)] = v_up[HUB_DEV * j : HUB_DEV * (j + 1), 0:LANES]
    x_mine[...] = rim_back[...]
    x_mine[0:16, :] = (rim_back[0:16, :].astype(F32) + v_hidden[0:16, :]).astype(BF16)
    last_copy = remote(x_mine, x_peer, peer_send.at[2], peer_recv.at[2], peer)
    last_copy.start()

    part_copy.wait_recv()
    v_direct[...] += p_mine[...].astype(F32) + p_peer[...].astype(F32)
    last_copy.wait_recv()
    extra = x_mine[...].astype(F32) + x_peer[...].astype(F32)
    o_grad[0:RIM, :] = (v_direct[0:RIM, :] + extra[0:RIM]).astype(BF16)
    o_grad[RIM : rows - RIM, :] = v_direct[RIM : rows - RIM, :].astype(BF16)
    o_grad[rows - RIM : rows, :] = (v_direct[rows - RIM : rows, :] + extra[RIM : 2 * RIM]).astype(BF16)
    store_grad = pltpu.make_async_copy(o_grad, out_grad, store_sem.at[2])
    store_grad.start()

    @pl.when(has_right)
    def _():
        to_right.wait_send()
        back_right.wait_send()

    @pl.when(has_left)
    def _():
        to_left.wait_send()
        back_left.wait_send()

    hub_wait(v_hub, hub_send.at[0])
    hub_wait(hub_out, hub_send.at[1])
    gather_copy.wait_send()
    part_copy.wait_send()
    last_copy.wait_send()
    store_nodes.wait()
    store_edges.wait()
    store_grad.wait()


def body(
    nodes, edges, senders, receivers, edge_proj, send_proj, recv_proj, edge_bias, edge_out, edge_gain, edge_shift,
    node_in, node_bias, node_out, node_gain, node_shift, node_cot,
):
    blocks = lax.axis_size("space")
    rows, width = nodes.shape
    count = edges.shape[0]
    tile = HUB_DEV * (width // LANES)
    late = 2 * RIM + HUB_DEV * blocks

    def line(vec):
        return vec.reshape(1, -1)

    args = (
        line(senders), line(receivers), nodes, edges, edge_proj, send_proj, recv_proj, line(edge_bias), edge_out,
        line(edge_gain), line(edge_shift), node_in, line(node_bias), node_out, line(node_gain), line(node_shift), node_cot,
    )
    any_spec = pl.BlockSpec(memory_space=pl.ANY)
    vmem = pltpu.VMEM
    dma = pltpu.SemaphoreType.DMA
    scratch = [vmem(a.shape, a.dtype) for a in args] + [
        vmem((late, width), BF16),
        vmem((tile, LANES), F32),
        vmem((blocks * tile, LANES), F32),
        vmem((count, rows), BF16),
        vmem((count, rows), BF16),
        vmem((count, late), BF16),
        vmem((count, width), F32),
        vmem((count, width), F32),
        vmem((count, width), BF16),
        vmem((count, width), F32),
        vmem((count, LANES), F32),
        vmem((count, width), BF16),
        vmem((rows, width), BF16),
        vmem((rows, width), BF16),
        vmem((rows, width), F32),
        vmem((rows, width), BF16),
        vmem((rows, width), F32),
        vmem((count, width), F32),
        vmem((count, width), BF16),
        vmem((count, width), BF16),
        vmem((2 * RIM, width), BF16),
        vmem((2 * RIM, width), BF16),
        vmem((blocks * tile, LANES), F32),
        vmem((blocks * tile, LANES), F32),
        vmem((rows, width), BF16),
        vmem((rows, width), BF16),
        vmem((2 * RIM, width), BF16),
        vmem((2 * RIM, width), BF16),
        vmem((rows, width), BF16),
        vmem((rows, width), BF16),
        vmem((count, width), BF16),
        dma((len(args),)),
        dma((3,)),
        dma((4,)),
        dma((4,)),
        dma((2,)),
        dma((2,)),
        dma((3,)),
        dma((3,)),
    ]
    return pl.pallas_call(
        functools.partial(kernel, blocks),
        out_shape=(
            jax.ShapeDtypeStruct((rows, width), BF16),
            jax.ShapeDtypeStruct((rows, width), BF16),
            jax.ShapeDtypeStruct((count, width), BF16),
        ),
        in_specs=[any_spec] * len(args),
        out_specs=(any_spec,) * 3,
        scratch_shapes=scratch,
        compiler_params=pltpu.CompilerParams(
            collective_id=0, has_side_effects=True, vmem_limit_bytes=60 * 1024 * 1024
        ),
    )(*args)


def solution(mesh):
    in_specs = (
        P("space", None),
        P(("space", "feat"), None),
        P(("space", "feat")),
        P(("space", "feat")),
        *([P()] * 12),
        P("space", None),
    )
    out_specs = (P("space", None), P("space", None), P(("space", "feat"), None))
    return jax.shard_map(body, mesh=mesh, in_specs=in_specs, out_specs=out_specs, check_vma=False)
```

```python
import functools

import jax
import jax.numpy as jnp
from jax import lax
from jax.experimental import pallas as pl
from jax.experimental.pallas import tpu as pltpu
from jax.sharding import PartitionSpec as P

RIM = 48
HUB_DEV = 2
LANES = 128
CHUNK = 64
epsilon = 1e-05

F32 = jnp.float32
BF16 = jnp.bfloat16
MESH = pl.DeviceIdType.MESH


def mm(a, b):
    return jnp.dot(a, b, preferred_element_type=F32)


def mm_t(a, b):
    return lax.dot_general(a, b, (((1,), (1,)), ((), ())), preferred_element_type=F32)


def sigmoid(v):
    return 0.5 * jnp.tanh(0.5 * v) + 0.5


def mean_row(v):
    return jnp.mean(v, axis=-1, keepdims=True)


def late_ids(index, own_block, blocks, rows):
    left = (own_block * rows - RIM) + index
    right = (own_block + 1) * rows + (index - RIM)
    hub = index - 2 * RIM
    row = jnp.zeros_like(hub)
    for step in range(1, HUB_DEV):
        row = row + jnp.where(hub >= step * blocks, 1, 0)
    block = hub - row * blocks
    hub_id = block * rows + row
    hub_id = jnp.where((block == own_block) | (block == own_block + 1), -1, hub_id)
    return jnp.where(index < RIM, left, jnp.where(index < 2 * RIM, right, hub_id))


def onehot(a, b):
    return jnp.where(a == b, 1.0, 0.0).astype(BF16)


def kernel(
    blocks,
    send_id, recv_id, nodes, edges, w_edge, w_send, w_recv, bias, w_out, gain_e, shift_e,
    w_in, bias_n, w_mix, gain_n, shift_n, cot,
    o_nodes, o_grad, o_edges,
    v_send_id, v_recv_id, v_nodes, v_edges, v_edge, v_send, v_recv, v_bias, v_out, v_gain_e, v_shift_e,
    v_in, v_bias_n, v_mix, v_gain_n, v_shift_n, v_cot,
    v_late, v_hub_src, v_hub, oh_own, oh_recv, oh_late,
    v_hidden, v_slope, v_act, v_normed, v_scale, v_new,
    g_mine, g_peer, v_pre, v_dpre, v_direct, v_up, v_dsum, v_edpre,
    rim_out, rim_back, hub_out, hub_back, p_mine, p_peer, x_mine, x_peer,
    load_sem, rim_send, rim_recv, hub_send, hub_recv, peer_send, peer_recv,
):
    me = lax.axis_index("space")
    core = lax.axis_index("feat")
    unroll = blocks - 1 if blocks <= 16 else 5
    rows, width = v_nodes.shape
    count = v_edges.shape[0]
    pieces = width // LANES
    tile = HUB_DEV * pieces
    peer = (me, 1 - core)
    left, right = (me - 1, core), (me + 1, core)
    has_left, has_right = me > 0, me < blocks - 1

    barrier = pltpu.get_barrier_semaphore()

    def greet(step, carry):
        other = lax.rem(me + step, blocks)
        pl.semaphore_signal(barrier, inc=1, device_id=(other, core), device_id_type=MESH)
        return carry

    lax.fori_loop(1, blocks, greet, 0, unroll=unroll)
    pl.semaphore_signal(barrier, inc=1, device_id=peer, device_id_type=MESH)

    pairs = [
        (nodes, v_nodes), (send_id, v_send_id), (recv_id, v_recv_id), (w_recv, v_recv), (w_send, v_send),
        (edges, v_edges), (w_edge, v_edge), (bias, v_bias), (w_out, v_out), (gain_e, v_gain_e), (shift_e, v_shift_e),
        (w_in, v_in), (bias_n, v_bias_n), (w_mix, v_mix), (gain_n, v_gain_n), (shift_n, v_shift_n), (cot, v_cot),
    ]
    loads = [pltpu.make_async_copy(src, dst, load_sem.at[k]) for k, (src, dst) in enumerate(pairs)]
    for load in loads:
        load.start()

    def ready(*refs):
        for k, (_, dst) in enumerate(pairs):
            if any(dst is ref for ref in refs):
                loads[k].wait()

    def remote(src, dst, send_sem, recv_sem, device):
        return pltpu.make_async_remote_copy(
            src_ref=src, dst_ref=dst, send_sem=send_sem, recv_sem=recv_sem, device_id=device, device_id_type=MESH
        )

    my_slot = pl.ds(pl.multiple_of(me * tile, tile), tile)

    def hub_copy(step, src, dst, kind):
        other = lax.rem(me + step, blocks)
        return remote(src(other), dst.at[my_slot], hub_send.at[kind], hub_recv.at[kind], (other, core))

    def hub_wait(buffer, sem):
        part = buffer.at[pl.ds(0, (blocks - 1) * tile)]
        pltpu.make_async_copy(part, part, sem).wait()

    ready(v_nodes)
    head = v_nodes[0:16, :].astype(F32)
    for j in range(pieces):
        v_hub_src[HUB_DEV * j : HUB_DEV * (j + 1), :] = head[0:HUB_DEV, LANES * j : LANES * (j + 1)]
    v_hub[my_slot, :] = v_hub_src[...]
    hub_back[my_slot, :] = jnp.zeros((tile, LANES), F32)
    zero_rim = jnp.zeros((RIM, width), BF16)

    @pl.when(jnp.logical_not(has_left))
    def _():
        v_late[0:RIM, :] = zero_rim
        rim_back[0:RIM, :] = zero_rim

    @pl.when(jnp.logical_not(has_right))
    def _():
        v_late[RIM : 2 * RIM, :] = zero_rim
        rim_back[RIM : 2 * RIM, :] = zero_rim

    pl.semaphore_wait(barrier, blocks)

    low, high = pl.ds(0, RIM), pl.ds(RIM, RIM)
    to_right = remote(nodes.at[pl.ds(rows - RIM, RIM)], v_late.at[low], rim_send.at[0], rim_recv.at[0], right)
    to_left = remote(nodes.at[pl.ds(0, RIM)], v_late.at[high], rim_send.at[1], rim_recv.at[1], left)

    @pl.when(has_right)
    def _():
        to_right.start()

    @pl.when(has_left)
    def _():
        to_left.start()

    def push_hub(step, carry):
        hub_copy(step, lambda other: v_hub_src, v_hub, 0).start()
        return carry

    lax.fori_loop(1, blocks, push_hub, 0, unroll=unroll)

    ready(v_send_id, v_recv_id)
    ids_s, ids_r = v_send_id[...].reshape(1, count), v_recv_id[...].reshape(1, count)
    col_s = jnp.transpose(jnp.broadcast_to(ids_s, (LANES, count)))[:, 0:1]
    col_r = jnp.transpose(jnp.broadcast_to(ids_r, (LANES, count)))[:, 0:1]
    own_ids = lax.broadcasted_iota(jnp.int32, (1, rows), 1) + me * rows
    late_count = v_late.shape[0]
    late_row = late_ids(lax.broadcasted_iota(jnp.int32, (1, late_count), 1), me, blocks, rows)
    oh_own[...] = onehot(col_s, own_ids)
    oh_recv[...] = onehot(col_r, own_ids)
    oh_late[...] = onehot(col_s, late_row)

    ready(v_recv, v_send)
    recv_terms = mm(v_nodes[...], v_recv[...]).astype(BF16)
    send_terms = mm(v_nodes[...], v_send[...]).astype(BF16)
    ready(v_edges, v_edge, v_bias)
    v_hidden[...] = (
        mm(v_edges[...], v_edge[...]) + mm(oh_recv[...], recv_terms) + mm(oh_own[...], send_terms) + v_bias[...]
    )

    @pl.when(has_left)
    def _():
        to_right.wait_recv()

    @pl.when(has_right)
    def _():
        to_left.wait_recv()

    hub_wait(v_hub, hub_recv.at[0])
    for r in range(HUB_DEV):
        for j in range(pieces):
            part = v_hub[pl.ds(HUB_DEV * j + r, blocks, stride=tile), :]
            v_late[2 * RIM + r * blocks : 2 * RIM + (r + 1) * blocks, LANES * j : LANES * (j + 1)] = part.astype(BF16)
    late_terms = mm(v_late[...], v_send[...]).astype(BF16)
    v_hidden[...] += mm(oh_late[...], late_terms)

    chunks = [pl.ds(start, CHUNK) for start in range(0, count, CHUNK)]
    for at in chunks:
        pre = v_hidden[at, :]
        sig = sigmoid(pre)
        act = pre * sig
        v_act[at, :] = act.astype(BF16)
        v_slope[at, :] = sig + act * (1.0 - sig)
    ready(v_out, v_gain_e, v_shift_e)
    v_hidden[...] = mm(v_act[...], v_out[...])
    for at in chunks:
        total = v_hidden[at, :]
        centred = total - mean_row(total)
        inv = lax.rsqrt(mean_row(centred * centred) + epsilon)
        normed = centred * inv
        v_normed[at, :] = normed
        v_scale[at, :] = jnp.broadcast_to(inv, (CHUNK, LANES))
        v_new[at, :] = (v_edges[at, :].astype(F32) + normed * v_gain_e[...] + v_shift_e[...]).astype(BF16)

    own_col = lax.broadcasted_iota(jnp.int32, (rows, 1), 0) + me * rows
    t_recv = onehot(own_col, ids_r)
    g_mine[...] = mm(t_recv, v_new[...]).astype(BF16)
    gather_copy = remote(g_mine, g_peer, peer_send.at[0], peer_recv.at[0], peer)
    gather_copy.start()

    ready(v_in, v_bias_n, v_mix, v_gain_n, v_shift_n, v_cot)
    v_pre[...] = mm(v_nodes[...], v_in[0:width, :]) + v_bias_n[...]
    gather_copy.wait_recv()
    gathered = (g_mine[...].astype(F32) + g_peer[...].astype(F32)).astype(BF16)
    pre = v_pre[...] + mm(gathered, v_in[width : 2 * width, :])
    sig = sigmoid(pre)
    act = pre * sig
    v_pre[...] = sig + act * (1.0 - sig)
    mix = mm(act.astype(BF16), v_mix[...])
    centred = mix - mean_row(mix)
    inv = lax.rsqrt(mean_row(centred * centred) + epsilon)
    normed = centred * inv
    o_nodes[...] = (v_nodes[...].astype(F32) + normed * v_gain_n[...] + v_shift_n[...]).astype(BF16)
    scaled = v_cot[...].astype(F32) * v_gain_n[...]
    dmix = (inv * (scaled - mean_row(scaled) - normed * mean_row(scaled * normed))).astype(BF16)
    v_dpre[...] = (mm_t(dmix, v_mix[...]) * v_pre[...]).astype(BF16)
    gathered_grad = mm_t(v_dpre[...], v_in[width : 2 * width, :]).astype(BF16)

    v_up[...] = mm(oh_recv[...], gathered_grad)
    for at in chunks:
        normed = v_normed[at, :]
        scaled = v_up[at, :] * v_gain_e[...]
        v_dsum[at, :] = (
            v_scale[at, 0:1] * (scaled - mean_row(scaled) - normed * mean_row(scaled * normed))
        ).astype(BF16)
    v_hidden[...] = mm_t(v_dsum[...], v_out[...])
    for at in chunks:
        v_edpre[at, :] = (v_hidden[at, :] * v_slope[at, :]).astype(BF16)

    late_col = late_ids(lax.broadcasted_iota(jnp.int32, (late_count, 1), 0), me, blocks, rows)
    t_late = onehot(late_col, ids_s)
    late_sums = mm(t_late, v_edpre[...]).astype(BF16)
    late_part = mm_t(late_sums, v_send[...])
    rim_out[...] = late_part[0 : 2 * RIM, :].astype(BF16)
    back_left = remote(rim_out.at[low], rim_back.at[high], rim_send.at[2], rim_recv.at[2], left)
    back_right = remote(rim_out.at[high], rim_back.at[low], rim_send.at[3], rim_recv.at[3], right)

    @pl.when(has_left)
    def _():
        back_left.start()

    @pl.when(has_right)
    def _():
        back_right.start()

    for r in range(HUB_DEV):
        for j in range(pieces):
            hub_out[pl.ds(HUB_DEV * j + r, blocks, stride=tile), :] = late_part[
                2 * RIM + r * blocks : 2 * RIM + (r + 1) * blocks, LANES * j : LANES * (j + 1)
            ]

    def hub_part(other):
        return hub_out.at[pl.ds(pl.multiple_of(other * tile, tile), tile)]

    def return_hub(step, carry):
        hub_copy(step, hub_part, hub_back, 1).start()
        return carry

    lax.fori_loop(1, blocks, return_hub, 0, unroll=unroll)

    t_own = onehot(own_col, ids_s)
    t_recv = onehot(own_col, ids_r)
    send_sums = mm(t_own, v_edpre[...]).astype(BF16)
    recv_sums = mm(t_recv, v_edpre[...]).astype(BF16)
    p_mine[...] = (mm_t(send_sums, v_send[...]) + mm_t(recv_sums, v_recv[...])).astype(BF16)
    part_copy = remote(p_mine, p_peer, peer_send.at[1], peer_recv.at[1], peer)
    part_copy.start()

    o_edges[...] = (v_up[...] + mm_t(v_edpre[...], v_edge[...])).astype(BF16)
    v_direct[...] = v_cot[...].astype(F32) + mm_t(v_dpre[...], v_in[0:width, :])

    @pl.when(has_right)
    def _():
        back_left.wait_recv()

    @pl.when(has_left)
    def _():
        back_right.wait_recv()

    hub_wait(hub_back, hub_recv.at[1])
    hub_sum = jnp.sum(hub_back[...].reshape(blocks, tile, LANES), axis=0)
    v_up[0:tile, 0:LANES] = hub_sum
    v_hidden[0:16, :] = jnp.zeros((16, width), F32)
    for j in range(pieces):
        v_hidden[0:HUB_DEV, LANES * j : LANES * (j + 1)] = v_up[HUB_DEV * j : HUB_DEV * (j + 1), 0:LANES]
    x_mine[...] = rim_back[...]
    x_mine[0:16, :] = (rim_back[0:16, :].astype(F32) + v_hidden[0:16, :]).astype(BF16)
    last_copy = remote(x_mine, x_peer, peer_send.at[2], peer_recv.at[2], peer)
    last_copy.start()

    part_copy.wait_recv()
    v_direct[...] += p_mine[...].astype(F32) + p_peer[...].astype(F32)
    last_copy.wait_recv()
    extra = x_mine[...].astype(F32) + x_peer[...].astype(F32)
    o_grad[0:RIM, :] = (v_direct[0:RIM, :] + extra[0:RIM]).astype(BF16)
    o_grad[RIM : rows - RIM, :] = v_direct[RIM : rows - RIM, :].astype(BF16)
    o_grad[rows - RIM : rows, :] = (v_direct[rows - RIM : rows, :] + extra[RIM : 2 * RIM]).astype(BF16)

    @pl.when(has_right)
    def _():
        to_right.wait_send()
        back_right.wait_send()

    @pl.when(has_left)
    def _():
        to_left.wait_send()
        back_left.wait_send()

    hub_wait(v_hub, hub_send.at[0])
    hub_wait(hub_out, hub_send.at[1])
    gather_copy.wait_send()
    part_copy.wait_send()
    last_copy.wait_send()


def store(*refs):
    sems = refs[-1]
    copies = [pltpu.make_async_copy(refs[k], refs[3 + k], sems.at[k]) for k in range(3)]
    for copy in copies:
        copy.start()
    for copy in copies:
        copy.wait()


def body(
    nodes, edges, senders, receivers, edge_proj, send_proj, recv_proj, edge_bias, edge_out, edge_gain, edge_shift,
    node_in, node_bias, node_out, node_gain, node_shift, node_cot,
):
    blocks = lax.axis_size("space")
    rows, width = nodes.shape
    count = edges.shape[0]
    tile = HUB_DEV * (width // LANES)
    late = 2 * RIM + HUB_DEV * blocks

    def line(vec):
        return vec.reshape(1, -1)

    args = (
        senders, receivers, nodes, edges, edge_proj, send_proj, recv_proj, line(edge_bias), edge_out,
        line(edge_gain), line(edge_shift), node_in, line(node_bias), node_out, line(node_gain), line(node_shift), node_cot,
    )
    any_spec = pl.BlockSpec(memory_space=pl.ANY)
    vmem = pltpu.VMEM
    dma = pltpu.SemaphoreType.DMA
    scratch = [vmem(a.shape, a.dtype) for a in args] + [
        vmem((late, width), BF16),
        vmem((tile, LANES), F32),
        vmem((blocks * tile, LANES), F32),
        vmem((count, rows), BF16),
        vmem((count, rows), BF16),
        vmem((count, late), BF16),
        vmem((count, width), F32),
        vmem((count, width), F32),
        vmem((count, width), BF16),
        vmem((count, width), F32),
        vmem((count, LANES), F32),
        vmem((count, width), BF16),
        vmem((rows, width), BF16),
        vmem((rows, width), BF16),
        vmem((rows, width), F32),
        vmem((rows, width), BF16),
        vmem((rows, width), F32),
        vmem((count, width), F32),
        vmem((count, width), BF16),
        vmem((count, width), BF16),
        vmem((2 * RIM, width), BF16),
        vmem((2 * RIM, width), BF16),
        vmem((blocks * tile, LANES), F32),
        vmem((blocks * tile, LANES), F32),
        vmem((rows, width), BF16),
        vmem((rows, width), BF16),
        vmem((2 * RIM, width), BF16),
        vmem((2 * RIM, width), BF16),
        dma((len(args),)),
        dma((4,)),
        dma((4,)),
        dma((2,)),
        dma((2,)),
        dma((3,)),
        dma((3,)),
    ]
    results = pl.pallas_call(
        functools.partial(kernel, blocks),
        out_shape=(
            pltpu.VMEM((rows, width), BF16),
            pltpu.VMEM((rows, width), BF16),
            pltpu.VMEM((count, width), BF16),
        ),
        in_specs=[any_spec] * len(args),
        out_specs=(pl.BlockSpec(memory_space=pltpu.VMEM),) * 3,
        scratch_shapes=scratch,
        compiler_params=pltpu.CompilerParams(
            collective_id=0, has_side_effects=True, vmem_limit_bytes=60 * 1024 * 1024
        ),
    )(*args)
    return pl.pallas_call(
        store,
        out_shape=tuple(jax.ShapeDtypeStruct(r.shape, r.dtype) for r in results),
        in_specs=[any_spec] * 3,
        out_specs=(any_spec,) * 3,
        scratch_shapes=[dma((3,))],
    )(*results)


def solution(mesh):
    in_specs = (
        P("space", None),
        P(("space", "feat"), None),
        P(("space", "feat")),
        P(("space", "feat")),
        *([P()] * 12),
        P("space", None),
    )
    out_specs = (P("space", None), P("space", None), P(("space", "feat"), None))
    return jax.shard_map(body, mesh=mesh, in_specs=in_specs, out_specs=out_specs, check_vma=False)
```

```python
import functools

import jax
import jax.numpy as jnp
from jax import lax
from jax.experimental import pallas as pl
from jax.experimental.pallas import tpu as pltpu
from jax.sharding import PartitionSpec as P

RIM = 48
HUB_DEV = 2
LANES = 128
CHUNK = 32
GROUPS = 2
epsilon = 1e-05

F32 = jnp.float32
BF16 = jnp.bfloat16
MESH = pl.DeviceIdType.MESH


def mm(a, b):
    return jnp.dot(a, b, preferred_element_type=F32)


def mm_t(a, b):
    return lax.dot_general(a, b, (((1,), (1,)), ((), ())), preferred_element_type=F32)


def sigmoid(v):
    return 0.5 * jnp.tanh(0.5 * v) + 0.5


def mean_row(v):
    return jnp.mean(v, axis=-1, keepdims=True)


def late_ids(index, own_block, blocks, rows):
    left = (own_block * rows - RIM) + index
    right = (own_block + 1) * rows + (index - RIM)
    hub = index - 2 * RIM
    row = jnp.zeros_like(hub)
    for step in range(1, HUB_DEV):
        row = row + jnp.where(hub >= step * blocks, 1, 0)
    block = hub - row * blocks
    hub_id = block * rows + row
    hub_id = jnp.where((block == own_block) | (block == own_block + 1), -1, hub_id)
    return jnp.where(index < RIM, left, jnp.where(index < 2 * RIM, right, hub_id))


def onehot(a, b):
    return jnp.where(a == b, 1.0, 0.0).astype(BF16)


def kernel(
    blocks,
    send_id, recv_id, nodes, edges, w_edge, w_send, w_recv, bias, w_out, gain_e, shift_e,
    w_in, bias_n, w_mix, gain_n, shift_n, cot,
    o_nodes, o_grad, o_edges,
    v_send_id, v_recv_id, v_nodes, v_edges, v_edge, v_send, v_recv, v_bias, v_out, v_gain_e, v_shift_e,
    v_in, v_bias_n, v_mix, v_gain_n, v_shift_n, v_cot,
    v_late, v_hub_src, v_hub, oh_own, oh_recv, oh_late,
    v_hidden, v_slope, v_act, v_normed, v_scale, v_new,
    g_mine, g_peer, v_pre, v_dpre, v_direct, v_up, v_dsum, v_edpre,
    terms, t_sums, t_late, v_sum, v_scaled, v_node_normed, v_up_scaled,
    rim_out, rim_back, hub_out, hub_back, p_mine, p_peer, x_mine, x_peer,
    load_sem, rim_send, rim_recv, hub_send, hub_recv, peer_send, peer_recv,
):
    me = lax.axis_index("space")
    core = lax.axis_index("feat")
    unroll = blocks - 1 if blocks <= 16 else 5
    rows, width = v_nodes.shape
    count = v_edges.shape[0]
    pieces = width // LANES
    tile = HUB_DEV * pieces
    peer = (me, 1 - core)
    left, right = (me - 1, core), (me + 1, core)
    has_left, has_right = me > 0, me < blocks - 1

    size = count // GROUPS
    groups = [pl.ds(start, size) for start in range(0, count, size)]

    def chunks(g):
        return [pl.ds(start, CHUNK) for start in range(g.start, g.start + size, CHUNK)]

    barrier = pltpu.get_barrier_semaphore()

    def greet(step, carry):
        other = lax.rem(me + step, blocks)
        pl.semaphore_signal(barrier, inc=1, device_id=(other, core), device_id_type=MESH)
        return carry

    lax.fori_loop(1, blocks, greet, 0, unroll=unroll)
    pl.semaphore_signal(barrier, inc=1, device_id=peer, device_id_type=MESH)

    pairs = [
        (nodes, v_nodes), (send_id, v_send_id), (recv_id, v_recv_id), (w_recv, v_recv), (w_send, v_send),
        (edges, v_edges), (w_edge, v_edge), (bias, v_bias), (w_out, v_out), (gain_e, v_gain_e), (shift_e, v_shift_e),
        (w_in, v_in), (bias_n, v_bias_n), (w_mix, v_mix), (gain_n, v_gain_n), (shift_n, v_shift_n), (cot, v_cot),
    ]
    loads = [pltpu.make_async_copy(src, dst, load_sem.at[k]) for k, (src, dst) in enumerate(pairs)]
    for load in loads:
        load.start()

    def ready(*refs):
        for k, (_, dst) in enumerate(pairs):
            if any(dst is ref for ref in refs):
                loads[k].wait()

    def remote(src, dst, send_sem, recv_sem, device):
        return pltpu.make_async_remote_copy(
            src_ref=src, dst_ref=dst, send_sem=send_sem, recv_sem=recv_sem, device_id=device, device_id_type=MESH
        )

    my_slot = pl.ds(pl.multiple_of(me * tile, tile), tile)

    def hub_copy(step, src, dst, kind):
        other = lax.rem(me + step, blocks)
        return remote(src(other), dst.at[my_slot], hub_send.at[kind], hub_recv.at[kind], (other, core))

    def hub_wait(buffer, sem):
        part = buffer.at[pl.ds(0, (blocks - 1) * tile)]
        pltpu.make_async_copy(part, part, sem).wait()

    ready(v_nodes)
    head = v_nodes[0:16, :].astype(F32)
    for j in range(pieces):
        v_hub_src[HUB_DEV * j : HUB_DEV * (j + 1), :] = head[0:HUB_DEV, LANES * j : LANES * (j + 1)]
    v_hub[my_slot, :] = v_hub_src[...]
    hub_back[my_slot, :] = jnp.zeros((tile, LANES), F32)
    zero_rim = jnp.zeros((RIM, width), BF16)

    @pl.when(jnp.logical_not(has_left))
    def _():
        v_late[0:RIM, :] = zero_rim
        rim_back[0:RIM, :] = zero_rim

    @pl.when(jnp.logical_not(has_right))
    def _():
        v_late[RIM : 2 * RIM, :] = zero_rim
        rim_back[RIM : 2 * RIM, :] = zero_rim

    pl.semaphore_wait(barrier, blocks)

    low, high = pl.ds(0, RIM), pl.ds(RIM, RIM)
    to_right = remote(nodes.at[pl.ds(rows - RIM, RIM)], v_late.at[low], rim_send.at[0], rim_recv.at[0], right)
    to_left = remote(nodes.at[pl.ds(0, RIM)], v_late.at[high], rim_send.at[1], rim_recv.at[1], left)

    @pl.when(has_right)
    def _():
        to_right.start()

    @pl.when(has_left)
    def _():
        to_left.start()

    def push_hub(step, carry):
        hub_copy(step, lambda other: v_hub_src, v_hub, 0).start()
        return carry

    lax.fori_loop(1, blocks, push_hub, 0, unroll=unroll)

    ready(v_send_id, v_recv_id)
    ids_s, ids_r = v_send_id[...].reshape(1, count), v_recv_id[...].reshape(1, count)
    col_s = jnp.transpose(jnp.broadcast_to(ids_s, (LANES, count)))[:, 0:1]
    col_r = jnp.transpose(jnp.broadcast_to(ids_r, (LANES, count)))[:, 0:1]
    own_ids = lax.broadcasted_iota(jnp.int32, (1, rows), 1) + me * rows
    late_count = v_late.shape[0]
    late_row = late_ids(lax.broadcasted_iota(jnp.int32, (1, late_count), 1), me, blocks, rows)
    own_col = lax.broadcasted_iota(jnp.int32, (rows, 1), 0) + me * rows
    late_col = late_ids(lax.broadcasted_iota(jnp.int32, (late_count, 1), 0), me, blocks, rows)
    both = lax.broadcasted_iota(jnp.int32, (1, 2 * rows), 1)
    is_recv = both < rows
    both_ids = jnp.where(is_recv, both, both - rows) + me * rows
    oh_own[...] = onehot(jnp.where(is_recv, col_r, col_s), both_ids)
    oh_recv[...] = onehot(col_r, own_ids)
    oh_late[...] = onehot(col_s, late_row)
    t_sums[0:rows, :] = onehot(own_col, ids_r)

    ready(v_recv, v_send)
    terms[0:rows, :] = mm(v_nodes[...], v_recv[...]).astype(BF16)
    terms[rows : 2 * rows, :] = mm(v_nodes[...], v_send[...]).astype(BF16)
    ready(v_edges, v_edge, v_bias)
    for g in groups:
        v_hidden[g, :] = mm(v_edges[g, :], v_edge[...]) + mm(oh_own[g, :], terms[...]) + v_bias[...]

    @pl.when(has_left)
    def _():
        to_right.wait_recv()

    @pl.when(has_right)
    def _():
        to_left.wait_recv()

    hub_wait(v_hub, hub_recv.at[0])
    for r in range(HUB_DEV):
        for j in range(pieces):
            part = v_hub[pl.ds(HUB_DEV * j + r, blocks, stride=tile), :]
            v_late[2 * RIM + r * blocks : 2 * RIM + (r + 1) * blocks, LANES * j : LANES * (j + 1)] = part.astype(BF16)
    late_terms = mm(v_late[...], v_send[...]).astype(BF16)
    for g in groups:
        v_hidden[g, :] += mm(oh_late[g, :], late_terms)
        for at in chunks(g):
            pre = v_hidden[at, :]
            sig = sigmoid(pre)
            act = pre * sig
            v_act[at, :] = act.astype(BF16)
            v_slope[at, :] = sig + act * (1.0 - sig)
    ready(v_out, v_gain_e, v_shift_e)
    for g in groups:
        v_sum[g, :] = mm(v_act[g, :], v_out[...])
        for at in chunks(g):
            total = v_sum[at, :]
            centred = total - mean_row(total)
            inv = lax.rsqrt(mean_row(centred * centred) + epsilon)
            normed = centred * inv
            v_normed[at, :] = normed
            v_scale[at, :] = jnp.broadcast_to(inv, (CHUNK, LANES))
            v_new[at, :] = (v_edges[at, :].astype(F32) + normed * v_gain_e[...] + v_shift_e[...]).astype(BF16)

    g_mine[...] = mm(t_sums[0:rows, :], v_new[...]).astype(BF16)
    gather_copy = remote(g_mine, g_peer, peer_send.at[0], peer_recv.at[0], peer)
    gather_copy.start()

    ready(v_in, v_bias_n, v_mix, v_gain_n, v_shift_n, v_cot)
    v_pre[...] = mm(v_nodes[...], v_in[0:width, :]) + v_bias_n[...]
    t_sums[rows : 2 * rows, :] = onehot(own_col, ids_s)
    t_late[...] = onehot(late_col, ids_s)
    scaled = v_cot[...].astype(F32) * v_gain_n[...]
    v_scaled[...] = scaled - mean_row(scaled)
    gather_copy.wait_recv()
    gathered = (g_mine[...].astype(F32) + g_peer[...].astype(F32)).astype(BF16)
    pre = v_pre[...] + mm(gathered, v_in[width : 2 * width, :])
    sig = sigmoid(pre)
    act = pre * sig
    v_pre[...] = sig + act * (1.0 - sig)
    mix = mm(act.astype(BF16), v_mix[...])
    centred = mix - mean_row(mix)
    inv = lax.rsqrt(mean_row(centred * centred) + epsilon)
    normed = centred * inv
    v_node_normed[...] = normed
    scaled = v_scaled[...]
    dmix = (inv * (scaled - normed * mean_row(scaled * normed))).astype(BF16)
    v_dpre[...] = (mm_t(dmix, v_mix[...]) * v_pre[...]).astype(BF16)
    gathered_grad = mm_t(v_dpre[...], v_in[width : 2 * width, :])
    v_up[...] = gathered_grad.astype(BF16)
    scaled = gathered_grad * v_gain_e[...]
    v_up_scaled[...] = (scaled - mean_row(scaled)).astype(BF16)

    for g in groups:
        v_sum[g, :] = mm(oh_recv[g, :], v_up_scaled[...])
        for at in chunks(g):
            normed = v_normed[at, :]
            scaled = v_sum[at, :]
            v_dsum[at, :] = (v_scale[at, 0:1] * (scaled - normed * mean_row(scaled * normed))).astype(BF16)
    for g in groups:
        v_hidden[g, :] = mm_t(v_dsum[g, :], v_out[...])
        for at in chunks(g):
            v_edpre[at, :] = (v_hidden[at, :] * v_slope[at, :]).astype(BF16)

    late_sums = mm(t_late[...], v_edpre[...]).astype(BF16)
    late_part = mm_t(late_sums, v_send[...])
    rim_out[...] = late_part[0 : 2 * RIM, :].astype(BF16)
    back_left = remote(rim_out.at[low], rim_back.at[high], rim_send.at[2], rim_recv.at[2], left)
    back_right = remote(rim_out.at[high], rim_back.at[low], rim_send.at[3], rim_recv.at[3], right)

    @pl.when(has_left)
    def _():
        back_left.start()

    @pl.when(has_right)
    def _():
        back_right.start()

    for r in range(HUB_DEV):
        for j in range(pieces):
            hub_out[pl.ds(HUB_DEV * j + r, blocks, stride=tile), :] = late_part[
                2 * RIM + r * blocks : 2 * RIM + (r + 1) * blocks, LANES * j : LANES * (j + 1)
            ]

    def hub_part(other):
        return hub_out.at[pl.ds(pl.multiple_of(other * tile, tile), tile)]

    def return_hub(step, carry):
        hub_copy(step, hub_part, hub_back, 1).start()
        return carry

    lax.fori_loop(1, blocks, return_hub, 0, unroll=unroll)

    sums = mm(t_sums[...], v_edpre[...]).astype(BF16)
    p_mine[...] = (mm_t(sums[0:rows], v_recv[...]) + mm_t(sums[rows : 2 * rows], v_send[...])).astype(BF16)
    part_copy = remote(p_mine, p_peer, peer_send.at[1], peer_recv.at[1], peer)
    part_copy.start()

    for g in groups:
        o_edges[g, :] = (mm(oh_recv[g, :], v_up[...]) + mm_t(v_edpre[g, :], v_edge[...])).astype(BF16)
    o_nodes[...] = (v_nodes[...].astype(F32) + v_node_normed[...] * v_gain_n[...] + v_shift_n[...]).astype(BF16)
    v_direct[...] = v_cot[...].astype(F32) + mm_t(v_dpre[...], v_in[0:width, :])

    @pl.when(has_right)
    def _():
        back_left.wait_recv()

    @pl.when(has_left)
    def _():
        back_right.wait_recv()

    hub_wait(hub_back, hub_recv.at[1])
    hub_sum = jnp.sum(hub_back[...].reshape(blocks, tile, LANES), axis=0)
    v_sum[0:tile, 0:LANES] = hub_sum
    v_hidden[0:16, :] = jnp.zeros((16, width), F32)
    for j in range(pieces):
        v_hidden[0:HUB_DEV, LANES * j : LANES * (j + 1)] = v_sum[HUB_DEV * j : HUB_DEV * (j + 1), 0:LANES]
    x_mine[...] = rim_back[...]
    x_mine[0:16, :] = (rim_back[0:16, :].astype(F32) + v_hidden[0:16, :]).astype(BF16)
    last_copy = remote(x_mine, x_peer, peer_send.at[2], peer_recv.at[2], peer)
    last_copy.start()

    part_copy.wait_recv()
    v_direct[...] += p_mine[...].astype(F32) + p_peer[...].astype(F32)
    last_copy.wait_recv()
    extra = x_mine[...].astype(F32) + x_peer[...].astype(F32)
    o_grad[0:RIM, :] = (v_direct[0:RIM, :] + extra[0:RIM]).astype(BF16)
    o_grad[RIM : rows - RIM, :] = v_direct[RIM : rows - RIM, :].astype(BF16)
    o_grad[rows - RIM : rows, :] = (v_direct[rows - RIM : rows, :] + extra[RIM : 2 * RIM]).astype(BF16)

    @pl.when(has_right)
    def _():
        to_right.wait_send()
        back_right.wait_send()

    @pl.when(has_left)
    def _():
        to_left.wait_send()
        back_left.wait_send()

    hub_wait(v_hub, hub_send.at[0])
    hub_wait(hub_out, hub_send.at[1])
    gather_copy.wait_send()
    part_copy.wait_send()
    last_copy.wait_send()


def store(*refs):
    sems = refs[-1]
    copies = [pltpu.make_async_copy(refs[k], refs[3 + k], sems.at[k]) for k in range(3)]
    for copy in copies:
        copy.start()
    for copy in copies:
        copy.wait()


def body(
    nodes, edges, senders, receivers, edge_proj, send_proj, recv_proj, edge_bias, edge_out, edge_gain, edge_shift,
    node_in, node_bias, node_out, node_gain, node_shift, node_cot,
):
    blocks = lax.axis_size("space")
    rows, width = nodes.shape
    count = edges.shape[0]
    tile = HUB_DEV * (width // LANES)
    late = 2 * RIM + HUB_DEV * blocks

    def line(vec):
        return vec.reshape(1, -1)

    args = (
        senders, receivers, nodes, edges, edge_proj, send_proj, recv_proj, line(edge_bias), edge_out,
        line(edge_gain), line(edge_shift), node_in, line(node_bias), node_out, line(node_gain), line(node_shift), node_cot,
    )
    any_spec = pl.BlockSpec(memory_space=pl.ANY)
    vmem = pltpu.VMEM
    dma = pltpu.SemaphoreType.DMA
    scratch = [vmem(a.shape, a.dtype) for a in args] + [
        vmem((late, width), BF16),
        vmem((tile, LANES), F32),
        vmem((blocks * tile, LANES), F32),
        vmem((count, 2 * rows), BF16),
        vmem((count, rows), BF16),
        vmem((count, late), BF16),
        vmem((count, width), F32),
        vmem((count, width), F32),
        vmem((count, width), BF16),
        vmem((count, width), F32),
        vmem((count, LANES), F32),
        vmem((count, width), BF16),
        vmem((rows, width), BF16),
        vmem((rows, width), BF16),
        vmem((rows, width), F32),
        vmem((rows, width), BF16),
        vmem((rows, width), F32),
        vmem((rows, width), BF16),
        vmem((count, width), BF16),
        vmem((count, width), BF16),
        vmem((2 * rows, width), BF16),
        vmem((2 * rows, count), BF16),
        vmem((late, count), BF16),
        vmem((count, width), F32),
        vmem((rows, width), F32),
        vmem((rows, width), F32),
        vmem((rows, width), BF16),
        vmem((2 * RIM, width), BF16),
        vmem((2 * RIM, width), BF16),
        vmem((blocks * tile, LANES), F32),
        vmem((blocks * tile, LANES), F32),
        vmem((rows, width), BF16),
        vmem((rows, width), BF16),
        vmem((2 * RIM, width), BF16),
        vmem((2 * RIM, width), BF16),
        dma((len(args),)),
        dma((4,)),
        dma((4,)),
        dma((2,)),
        dma((2,)),
        dma((3,)),
        dma((3,)),
    ]
    results = pl.pallas_call(
        functools.partial(kernel, blocks),
        out_shape=(
            pltpu.VMEM((rows, width), BF16),
            pltpu.VMEM((rows, width), BF16),
            pltpu.VMEM((count, width), BF16),
        ),
        in_specs=[any_spec] * len(args),
        out_specs=(pl.BlockSpec(memory_space=pltpu.VMEM),) * 3,
        scratch_shapes=scratch,
        compiler_params=pltpu.CompilerParams(
            collective_id=0, has_side_effects=True, vmem_limit_bytes=60 * 1024 * 1024
        ),
    )(*args)
    return pl.pallas_call(
        store,
        out_shape=tuple(jax.ShapeDtypeStruct(r.shape, r.dtype) for r in results),
        in_specs=[any_spec] * 3,
        out_specs=(any_spec,) * 3,
        scratch_shapes=[dma((3,))],
        compiler_params=pltpu.CompilerParams(vmem_limit_bytes=2 * 1024 * 1024),
    )(*results)


def solution(mesh):
    in_specs = (
        P("space", None),
        P(("space", "feat"), None),
        P(("space", "feat")),
        P(("space", "feat")),
        *([P()] * 12),
        P("space", None),
    )
    out_specs = (P("space", None), P("space", None), P(("space", "feat"), None))
    return jax.shard_map(body, mesh=mesh, in_specs=in_specs, out_specs=out_specs, check_vma=False)
```

```python
import functools

import jax
import jax.numpy as jnp
from jax import lax
from jax.experimental import pallas as pl
from jax.experimental.pallas import tpu as pltpu
from jax.sharding import PartitionSpec as P

RIM = 48
HUB_DEV = 2
LANES = 128
CHUNK = 32
GROUPS = 2
epsilon = 1e-05

F32 = jnp.float32
BF16 = jnp.bfloat16
MESH = pl.DeviceIdType.MESH


def mm(a, b):
    return jnp.dot(a, b, preferred_element_type=F32)


def mm_t(a, b):
    return lax.dot_general(a, b, (((1,), (1,)), ((), ())), preferred_element_type=F32)


def sigmoid(v):
    return 0.5 * jnp.tanh(0.5 * v) + 0.5


def mean_row(v):
    return jnp.mean(v, axis=-1, keepdims=True)


def late_ids(index, own_block, blocks, rows):
    left = (own_block * rows - RIM) + index
    right = (own_block + 1) * rows + (index - RIM)
    hub = index - 2 * RIM
    row = jnp.zeros_like(hub)
    for step in range(1, HUB_DEV):
        row = row + jnp.where(hub >= step * blocks, 1, 0)
    block = hub - row * blocks
    hub_id = block * rows + row
    hub_id = jnp.where((block == own_block) | (block == own_block + 1), -1, hub_id)
    return jnp.where(index < RIM, left, jnp.where(index < 2 * RIM, right, hub_id))


def onehot(a, b):
    return jnp.where(a == b, 1.0, 0.0).astype(BF16)


def kernel(
    blocks,
    send_id, recv_id, nodes, edges, w_edge, w_send, w_recv, bias, w_out, gain_e, shift_e,
    w_in, bias_n, w_mix, gain_n, shift_n, cot,
    o_nodes, o_grad, o_edges,
    v_send_id, v_recv_id, v_nodes, v_edges, v_edge, v_send, v_recv, v_bias, v_out, v_gain_e, v_shift_e,
    v_in, v_bias_n, v_mix, v_gain_n, v_shift_n, v_cot,
    v_late, v_hub_src, v_hub, oh_own, oh_recv, oh_late,
    v_hidden, v_slope, v_act, v_normed, v_scale, v_new,
    g_mine, g_peer, v_pre, v_dpre, v_direct, v_up, v_dsum, v_edpre,
    terms, t_sums, t_late, v_sum, v_scaled, v_node_normed, v_up_scaled,
    rim_out, rim_back, hub_out, hub_back, p_mine, p_peer, e_mine, e_peer, v_head,
    load_sem, head_sem, rim_send, rim_recv, hub_send, hub_recv, peer_send, peer_recv,
):
    me = lax.axis_index("space")
    core = lax.axis_index("feat")
    unroll = blocks - 1 if blocks <= 16 else 5
    rows, width = v_nodes.shape
    count = v_edges.shape[0]
    pieces = width // LANES
    tile = HUB_DEV * pieces
    peer = (me, 1 - core)
    left, right = (me - 1, core), (me + 1, core)
    has_left, has_right = me > 0, me < blocks - 1

    size = count // GROUPS
    groups = [pl.ds(start, size) for start in range(0, count, size)]

    def chunks(g):
        return [pl.ds(start, CHUNK) for start in range(g.start, g.start + size, CHUNK)]

    head_load = pltpu.make_async_copy(nodes.at[pl.ds(0, 16)], v_head, head_sem.at[0])
    head_load.start()
    barrier = pltpu.get_barrier_semaphore()

    def hello(device):
        pl.semaphore_signal(barrier, inc=1, device_id=device, device_id_type=MESH)

    def greet(step, carry):
        hello((lax.rem(me + step, blocks), core))
        return carry

    lax.fori_loop(1, blocks, greet, 0, unroll=unroll)
    hello(peer)

    @pl.when(has_left)
    def _():
        hello((me - 1, 1 - core))

    @pl.when(has_right)
    def _():
        hello((me + 1, 1 - core))

    pairs = [
        (nodes, v_nodes), (send_id, v_send_id), (recv_id, v_recv_id), (w_recv, v_recv), (w_send, v_send),
        (edges, v_edges), (w_edge, v_edge), (bias, v_bias), (w_out, v_out), (gain_e, v_gain_e), (shift_e, v_shift_e),
        (w_in, v_in), (bias_n, v_bias_n), (w_mix, v_mix), (gain_n, v_gain_n), (shift_n, v_shift_n), (cot, v_cot),
    ]
    loads = [pltpu.make_async_copy(src, dst, load_sem.at[k]) for k, (src, dst) in enumerate(pairs)]
    for load in loads[:5]:
        load.start()

    def ready(*refs):
        for k, (_, dst) in enumerate(pairs):
            if any(dst is ref for ref in refs):
                loads[k].wait()

    def remote(src, dst, send_sem, recv_sem, device):
        return pltpu.make_async_remote_copy(
            src_ref=src, dst_ref=dst, send_sem=send_sem, recv_sem=recv_sem, device_id=device, device_id_type=MESH
        )

    my_slot = pl.ds(pl.multiple_of(me * tile, tile), tile)

    def hub_copy(step, src, dst, kind):
        other = lax.rem(me + step, blocks)
        return remote(src(other), dst.at[my_slot], hub_send.at[kind], hub_recv.at[kind], (other, core))

    def hub_wait(buffer, sem):
        part = buffer.at[pl.ds(0, (blocks - 1) * tile)]
        pltpu.make_async_copy(part, part, sem).wait()

    head_load.wait()
    head = v_head[...].astype(F32)
    for j in range(pieces):
        v_hub_src[HUB_DEV * j : HUB_DEV * (j + 1), :] = head[0:HUB_DEV, LANES * j : LANES * (j + 1)]
    v_hub[my_slot, :] = v_hub_src[...]
    hub_back[my_slot, :] = jnp.zeros((tile, LANES), F32)
    zero_rim = jnp.zeros((RIM, width), BF16)

    @pl.when(jnp.logical_not(has_left))
    def _():
        v_late[0:RIM, :] = zero_rim
        rim_back[0:RIM, :] = zero_rim

    @pl.when(jnp.logical_not(has_right))
    def _():
        v_late[RIM : 2 * RIM, :] = zero_rim
        rim_back[RIM : 2 * RIM, :] = zero_rim

    pl.semaphore_wait(barrier, blocks + jnp.where(has_left, 1, 0) + jnp.where(has_right, 1, 0))

    low, high = pl.ds(0, RIM), pl.ds(RIM, RIM)
    to_right = remote(nodes.at[pl.ds(rows - RIM, RIM)], v_late.at[low], rim_send.at[0], rim_recv.at[0], right)
    to_left = remote(nodes.at[pl.ds(0, RIM)], v_late.at[high], rim_send.at[1], rim_recv.at[1], left)

    @pl.when(has_right)
    def _():
        to_right.start()

    @pl.when(has_left)
    def _():
        to_left.start()

    def push_hub(step, carry):
        hub_copy(step, lambda other: v_hub_src, v_hub, 0).start()
        return carry

    lax.fori_loop(1, blocks, push_hub, 0, unroll=unroll)

    for load in loads[5:]:
        load.start()

    ready(v_send_id, v_recv_id)
    ids_s, ids_r = v_send_id[...].reshape(1, count), v_recv_id[...].reshape(1, count)
    col_s = jnp.transpose(jnp.broadcast_to(ids_s, (LANES, count)))[:, 0:1]
    col_r = jnp.transpose(jnp.broadcast_to(ids_r, (LANES, count)))[:, 0:1]
    own_ids = lax.broadcasted_iota(jnp.int32, (1, rows), 1) + me * rows
    late_count = v_late.shape[0]
    late_row = late_ids(lax.broadcasted_iota(jnp.int32, (1, late_count), 1), me, blocks, rows)
    own_col = lax.broadcasted_iota(jnp.int32, (rows, 1), 0) + me * rows
    late_col = late_ids(lax.broadcasted_iota(jnp.int32, (late_count, 1), 0), me, blocks, rows)
    both = lax.broadcasted_iota(jnp.int32, (1, 2 * rows), 1)
    is_recv = both < rows
    both_ids = jnp.where(is_recv, both, both - rows) + me * rows
    oh_own[...] = onehot(jnp.where(is_recv, col_r, col_s), both_ids)
    oh_recv[...] = onehot(col_r, own_ids)
    oh_late[...] = onehot(col_s, late_row)
    t_sums[0:rows, :] = onehot(own_col, ids_r)

    ready(v_nodes, v_recv, v_send)
    terms[0:rows, :] = mm(v_nodes[...], v_recv[...]).astype(BF16)
    terms[rows : 2 * rows, :] = mm(v_nodes[...], v_send[...]).astype(BF16)
    ready(v_edges, v_edge, v_bias)
    for g in groups:
        v_hidden[g, :] = mm(v_edges[g, :], v_edge[...]) + mm(oh_own[g, :], terms[...]) + v_bias[...]

    @pl.when(has_left)
    def _():
        to_right.wait_recv()

    @pl.when(has_right)
    def _():
        to_left.wait_recv()

    hub_wait(v_hub, hub_recv.at[0])
    for r in range(HUB_DEV):
        for j in range(pieces):
            part = v_hub[pl.ds(HUB_DEV * j + r, blocks, stride=tile), :]
            v_late[2 * RIM + r * blocks : 2 * RIM + (r + 1) * blocks, LANES * j : LANES * (j + 1)] = part.astype(BF16)
    late_terms = mm(v_late[...], v_send[...]).astype(BF16)
    for g in groups:
        v_hidden[g, :] += mm(oh_late[g, :], late_terms)
        for at in chunks(g):
            pre = v_hidden[at, :]
            sig = sigmoid(pre)
            act = pre * sig
            v_act[at, :] = act.astype(BF16)
            v_slope[at, :] = sig + act * (1.0 - sig)
    ready(v_out, v_gain_e, v_shift_e)
    for g in groups:
        v_sum[g, :] = mm(v_act[g, :], v_out[...])
        for at in chunks(g):
            total = v_sum[at, :]
            centred = total - mean_row(total)
            inv = lax.rsqrt(mean_row(centred * centred) + epsilon)
            normed = centred * inv
            v_normed[at, :] = normed
            v_scale[at, :] = jnp.broadcast_to(inv, (CHUNK, LANES))
            v_new[at, :] = (v_edges[at, :].astype(F32) + normed * v_gain_e[...] + v_shift_e[...]).astype(BF16)

    g_mine[...] = mm(t_sums[0:rows, :], v_new[...]).astype(BF16)
    gather_copy = remote(g_mine, g_peer, peer_send.at[0], peer_recv.at[0], peer)
    gather_copy.start()

    ready(v_in, v_bias_n, v_mix, v_gain_n, v_shift_n, v_cot)
    v_pre[...] = mm(v_nodes[...], v_in[0:width, :]) + v_bias_n[...]
    t_sums[rows : 2 * rows, :] = onehot(own_col, ids_s)
    t_late[...] = onehot(late_col, ids_s)
    scaled = v_cot[...].astype(F32) * v_gain_n[...]
    v_scaled[...] = scaled - mean_row(scaled)
    gather_copy.wait_recv()
    gathered = (g_mine[...].astype(F32) + g_peer[...].astype(F32)).astype(BF16)
    pre = v_pre[...] + mm(gathered, v_in[width : 2 * width, :])
    sig = sigmoid(pre)
    act = pre * sig
    v_pre[...] = sig + act * (1.0 - sig)
    mix = mm(act.astype(BF16), v_mix[...])
    centred = mix - mean_row(mix)
    inv = lax.rsqrt(mean_row(centred * centred) + epsilon)
    normed = centred * inv
    v_node_normed[...] = normed
    scaled = v_scaled[...]
    dmix = (inv * (scaled - normed * mean_row(scaled * normed))).astype(BF16)
    v_dpre[...] = (mm_t(dmix, v_mix[...]) * v_pre[...]).astype(BF16)
    gathered_grad = mm_t(v_dpre[...], v_in[width : 2 * width, :])
    v_up[...] = gathered_grad.astype(BF16)
    scaled = gathered_grad * v_gain_e[...]
    v_up_scaled[...] = (scaled - mean_row(scaled)).astype(BF16)

    for g in groups:
        v_sum[g, :] = mm(oh_recv[g, :], v_up_scaled[...])
        for at in chunks(g):
            normed = v_normed[at, :]
            scaled = v_sum[at, :]
            v_dsum[at, :] = (v_scale[at, 0:1] * (scaled - normed * mean_row(scaled * normed))).astype(BF16)
    for g in groups:
        v_hidden[g, :] = mm_t(v_dsum[g, :], v_out[...])
        for at in chunks(g):
            v_edpre[at, :] = (v_hidden[at, :] * v_slope[at, :]).astype(BF16)

    late_sums = mm(t_late[...], v_edpre[...]).astype(BF16)
    late_part = mm_t(late_sums, v_send[...])
    e_mine[...] = late_part.astype(BF16)
    late_copy = remote(e_mine, e_peer, peer_send.at[2], peer_recv.at[2], peer)
    late_copy.start()
    sums = mm(t_sums[...], v_edpre[...]).astype(BF16)
    p_mine[...] = (mm_t(sums[0:rows], v_recv[...]) + mm_t(sums[rows : 2 * rows], v_send[...])).astype(BF16)
    part_copy = remote(p_mine, p_peer, peer_send.at[1], peer_recv.at[1], peer)
    part_copy.start()
    late_copy.wait_recv()
    rim_out[...] = (e_mine[0 : 2 * RIM, :].astype(F32) + e_peer[0 : 2 * RIM, :].astype(F32)).astype(BF16)
    half = width // 2
    my_cols = pl.ds(pl.multiple_of(core * half, half), half)

    def back(src, dst, first, device, k):
        return remote(
            rim_out.at[src, my_cols], rim_back.at[dst, my_cols], rim_send.at[first + k], rim_recv.at[first + core], device
        )

    back_left = [back(low, high, 2, (me - 1, k), k) for k in range(2)]
    back_right = [back(high, low, 4, (me + 1, k), k) for k in range(2)]

    @pl.when(has_left)
    def _():
        for copy in back_left:
            copy.start()

    @pl.when(has_right)
    def _():
        for copy in back_right:
            copy.start()

    hub_part = e_mine[2 * RIM :, :].astype(F32) + e_peer[2 * RIM :, :].astype(F32)
    for r in range(HUB_DEV):
        for j in range(pieces):
            hub_out[pl.ds(HUB_DEV * j + r, blocks, stride=tile), :] = hub_part[
                r * blocks : (r + 1) * blocks, LANES * j : LANES * (j + 1)
            ]

    def hub_tile(other):
        return hub_out.at[pl.ds(pl.multiple_of(other * tile, tile), tile)]

    def return_hub(step, carry):
        hub_copy(step, hub_tile, hub_back, 1).start()
        return carry

    lax.fori_loop(1, blocks, return_hub, 0, unroll=unroll)

    for g in groups:
        o_edges[g, :] = (mm(oh_recv[g, :], v_up[...]) + mm_t(v_edpre[g, :], v_edge[...])).astype(BF16)
    o_nodes[...] = (v_nodes[...].astype(F32) + v_node_normed[...] * v_gain_n[...] + v_shift_n[...]).astype(BF16)
    v_direct[...] = v_cot[...].astype(F32) + mm_t(v_dpre[...], v_in[0:width, :])

    part_copy.wait_recv()
    v_direct[...] += p_mine[...].astype(F32) + p_peer[...].astype(F32)

    def landed(dst, first):
        for k in range(2):
            part = rim_back.at[dst, pl.ds(k * half, half)]
            remote(part, part, rim_send.at[first + k], rim_recv.at[first + k], peer).wait_recv()

    @pl.when(has_right)
    def _():
        landed(high, 2)

    @pl.when(has_left)
    def _():
        landed(low, 4)

    o_grad[RIM : rows - RIM, :] = v_direct[RIM : rows - RIM, :].astype(BF16)
    o_grad[rows - RIM : rows, :] = (v_direct[rows - RIM : rows, :] + rim_back[high, :].astype(F32)).astype(BF16)
    v_direct[0:RIM, :] += rim_back[low, :].astype(F32)
    hub_wait(hub_back, hub_recv.at[1])
    hub_wait(v_hub, hub_send.at[0])
    v_hub_src[...] = jnp.sum(hub_back[...].reshape(blocks, tile, LANES), axis=0)
    for j in range(pieces):
        v_direct[0:HUB_DEV, LANES * j : LANES * (j + 1)] += v_hub_src[HUB_DEV * j : HUB_DEV * (j + 1), :]
    o_grad[0:RIM, :] = v_direct[0:RIM, :].astype(BF16)

    @pl.when(has_right)
    def _():
        to_right.wait_send()
        for copy in back_right:
            copy.wait_send()

    @pl.when(has_left)
    def _():
        to_left.wait_send()
        for copy in back_left:
            copy.wait_send()

    hub_wait(hub_out, hub_send.at[1])
    gather_copy.wait_send()
    part_copy.wait_send()
    late_copy.wait_send()


def store(*refs):
    sems = refs[-1]
    copies = [pltpu.make_async_copy(refs[k], refs[3 + k], sems.at[k]) for k in range(3)]
    for copy in copies:
        copy.start()
    for copy in copies:
        copy.wait()


def body(
    nodes, edges, senders, receivers, edge_proj, send_proj, recv_proj, edge_bias, edge_out, edge_gain, edge_shift,
    node_in, node_bias, node_out, node_gain, node_shift, node_cot,
):
    blocks = lax.axis_size("space")
    rows, width = nodes.shape
    count = edges.shape[0]
    tile = HUB_DEV * (width // LANES)
    late = 2 * RIM + HUB_DEV * blocks

    def line(vec):
        return vec.reshape(1, -1)

    args = (
        senders, receivers, nodes, edges, edge_proj, send_proj, recv_proj, line(edge_bias), edge_out,
        line(edge_gain), line(edge_shift), node_in, line(node_bias), node_out, line(node_gain), line(node_shift), node_cot,
    )
    any_spec = pl.BlockSpec(memory_space=pl.ANY)
    vmem = pltpu.VMEM
    dma = pltpu.SemaphoreType.DMA
    scratch = [vmem(a.shape, a.dtype) for a in args] + [
        vmem((late, width), BF16),
        vmem((tile, LANES), F32),
        vmem((blocks * tile, LANES), F32),
        vmem((count, 2 * rows), BF16),
        vmem((count, rows), BF16),
        vmem((count, late), BF16),
        vmem((count, width), F32),
        vmem((count, width), F32),
        vmem((count, width), BF16),
        vmem((count, width), F32),
        vmem((count, LANES), F32),
        vmem((count, width), BF16),
        vmem((rows, width), BF16),
        vmem((rows, width), BF16),
        vmem((rows, width), F32),
        vmem((rows, width), BF16),
        vmem((rows, width), F32),
        vmem((rows, width), BF16),
        vmem((count, width), BF16),
        vmem((count, width), BF16),
        vmem((2 * rows, width), BF16),
        vmem((2 * rows, count), BF16),
        vmem((late, count), BF16),
        vmem((count, width), F32),
        vmem((rows, width), F32),
        vmem((rows, width), F32),
        vmem((rows, width), BF16),
        vmem((2 * RIM, width), BF16),
        vmem((2 * RIM, width), BF16),
        vmem((blocks * tile, LANES), F32),
        vmem((blocks * tile, LANES), F32),
        vmem((rows, width), BF16),
        vmem((rows, width), BF16),
        vmem((late, width), BF16),
        vmem((late, width), BF16),
        vmem((16, width), BF16),
        dma((len(args),)),
        dma((1,)),
        dma((6,)),
        dma((6,)),
        dma((2,)),
        dma((2,)),
        dma((3,)),
        dma((3,)),
    ]
    results = pl.pallas_call(
        functools.partial(kernel, blocks),
        out_shape=(
            pltpu.VMEM((rows, width), BF16),
            pltpu.VMEM((rows, width), BF16),
            pltpu.VMEM((count, width), BF16),
        ),
        in_specs=[any_spec] * len(args),
        out_specs=(pl.BlockSpec(memory_space=pltpu.VMEM),) * 3,
        scratch_shapes=scratch,
        compiler_params=pltpu.CompilerParams(
            collective_id=0, has_side_effects=True, vmem_limit_bytes=60 * 1024 * 1024
        ),
    )(*args)
    return pl.pallas_call(
        store,
        out_shape=tuple(jax.ShapeDtypeStruct(r.shape, r.dtype) for r in results),
        in_specs=[any_spec] * 3,
        out_specs=(any_spec,) * 3,
        scratch_shapes=[dma((3,))],
        compiler_params=pltpu.CompilerParams(vmem_limit_bytes=2 * 1024 * 1024),
    )(*results)


def solution(mesh):
    in_specs = (
        P("space", None),
        P(("space", "feat"), None),
        P(("space", "feat")),
        P(("space", "feat")),
        *([P()] * 12),
        P("space", None),
    )
    out_specs = (P("space", None), P("space", None), P(("space", "feat"), None))
    return jax.shard_map(body, mesh=mesh, in_specs=in_specs, out_specs=out_specs, check_vma=False)
```

```python
import functools

import jax
import jax.numpy as jnp
from jax import lax
from jax.experimental import pallas as pl
from jax.experimental.pallas import tpu as pltpu
from jax.sharding import PartitionSpec as P

RIM = 48
HUB_DEV = 2
LANES = 128
CHUNK = 32
GROUPS = 2
epsilon = 1e-05

F32 = jnp.float32
BF16 = jnp.bfloat16
MESH = pl.DeviceIdType.MESH


def mm(a, b):
    return jnp.dot(a, b, preferred_element_type=F32)


def mm_t(a, b):
    return lax.dot_general(a, b, (((1,), (1,)), ((), ())), preferred_element_type=F32)


def sigmoid(v):
    return 0.5 * jnp.tanh(0.5 * v) + 0.5


def mean_row(v):
    return jnp.mean(v, axis=-1, keepdims=True)


def late_ids(index, own_block, blocks, rows):
    left = (own_block * rows - RIM) + index
    right = (own_block + 1) * rows + (index - RIM)
    hub = index - 2 * RIM
    row = jnp.zeros_like(hub)
    for step in range(1, HUB_DEV):
        row = row + jnp.where(hub >= step * blocks, 1, 0)
    block = hub - row * blocks
    hub_id = block * rows + row
    hub_id = jnp.where((block == own_block) | (block == own_block + 1), -1, hub_id)
    return jnp.where(index < RIM, left, jnp.where(index < 2 * RIM, right, hub_id))


def onehot(a, b):
    return jnp.where(a == b, 1.0, 0.0).astype(BF16)


def kernel(
    blocks,
    send_id, recv_id, nodes, edges, w_edge, w_send, w_recv, bias, w_out, gain_e, shift_e,
    w_in, bias_n, w_mix, gain_n, shift_n, cot,
    o_nodes, o_grad, o_edges,
    v_send_id, v_recv_id, v_nodes, v_edges, v_edge, v_send, v_recv, v_bias, v_out, v_gain_e, v_shift_e,
    v_in, v_bias_n, v_mix, v_gain_n, v_shift_n, v_cot,
    v_late, v_hub_src, v_hub, oh_own, oh_recv, oh_late,
    v_hidden, v_slope, v_act, v_normed, v_scale, v_new,
    g_mine, g_peer, v_pre, v_dpre, v_direct, v_up, v_dsum, v_edpre,
    terms, t_sums, t_late, v_sum, v_scaled, v_node_normed, v_up_scaled,
    rim_out, rim_back, hub_out, hub_back, p_mine, p_peer, e_mine, e_peer, v_head,
    h_mine, h_peer, s_mine, s_peer,
    load_sem, head_sem, rim_send, rim_recv, hub_send, hub_recv, peer_send, peer_recv,
):
    me = lax.axis_index("space")
    core = lax.axis_index("feat")
    unroll = 5 if blocks > 16 else True
    rows, width = v_nodes.shape
    half = width // 2
    my_cols = pl.ds(pl.multiple_of(core * half, half), half)
    count = v_edges.shape[0]
    pieces = width // LANES
    tile = HUB_DEV * pieces
    peer = (me, 1 - core)
    left, right = (me - 1, core), (me + 1, core)
    has_left, has_right = me > 0, me < blocks - 1

    size = count // GROUPS
    groups = [pl.ds(start, size) for start in range(0, count, size)]

    def chunks(g):
        return [pl.ds(start, CHUNK) for start in range(g.start, g.start + size, CHUNK)]

    head_load = pltpu.make_async_copy(nodes.at[pl.ds(0, 16)], v_head, head_sem.at[0])
    head_load.start()
    v_hub[...] = jnp.zeros_like(v_hub)
    hub_back[...] = jnp.zeros_like(hub_back)
    zero_rim = jnp.zeros((RIM, width), BF16)

    @pl.when(jnp.logical_not(has_left))
    def _():
        v_late[0:RIM, :] = zero_rim
        rim_back[0:RIM, :] = zero_rim

    @pl.when(jnp.logical_not(has_right))
    def _():
        v_late[RIM : 2 * RIM, :] = zero_rim
        rim_back[RIM : 2 * RIM, :] = zero_rim

    barrier = pltpu.get_barrier_semaphore()

    def hello(device):
        pl.semaphore_signal(barrier, inc=1, device_id=device, device_id_type=MESH)

    def greet(step, carry):
        hello((lax.rem(me + step, blocks), core))
        return carry

    lax.fori_loop(1, blocks, greet, 0, unroll=unroll)
    hello(peer)

    pairs = [
        (nodes, v_nodes), (send_id, v_send_id), (recv_id, v_recv_id), (w_recv, v_recv), (w_send, v_send),
        (edges, v_edges), (w_edge, v_edge), (bias, v_bias), (w_out, v_out), (gain_e, v_gain_e), (shift_e, v_shift_e),
        (w_in, v_in), (bias_n, v_bias_n), (w_mix, v_mix), (gain_n, v_gain_n), (shift_n, v_shift_n), (cot, v_cot),
    ]
    loads = [pltpu.make_async_copy(src, dst, load_sem.at[k]) for k, (src, dst) in enumerate(pairs)]
    for load in loads[:5]:
        load.start()

    def ready(*refs):
        for k, (_, dst) in enumerate(pairs):
            if any(dst is ref for ref in refs):
                loads[k].wait()

    def remote(src, dst, send_sem, recv_sem, device):
        return pltpu.make_async_remote_copy(
            src_ref=src, dst_ref=dst, send_sem=send_sem, recv_sem=recv_sem, device_id=device, device_id_type=MESH
        )

    my_slot = pl.ds(pl.multiple_of(me * tile, tile), tile)

    def hub_copies(src, dst, kind):
        def push(turn, carry):
            other = lax.rem(me + 2 * turn + 2 - core, blocks)
            remote(src(other), dst.at[my_slot], hub_send.at[kind], hub_recv.at[kind], (other, core)).start()
            return carry

        lax.fori_loop(0, (blocks - 1) // 2, push, 0, unroll=unroll)
        if blocks % 2 == 0:

            @pl.when(core == 1)
            def _():
                push((blocks - 1) // 2, 0)

    def hub_wait(buffer, sem):
        for c in range(2):

            @pl.when(core == c)
            def _():
                part = buffer.at[pl.ds(0, ((blocks - 1 + c) // 2) * tile)]
                pltpu.make_async_copy(part, part, sem).wait()

    head_load.wait()
    head = v_head[...].astype(F32)
    for j in range(pieces):
        v_hub_src[HUB_DEV * j : HUB_DEV * (j + 1), :] = head[0:HUB_DEV, LANES * j : LANES * (j + 1)]
    pl.semaphore_wait(barrier, blocks)

    low, high = pl.ds(0, RIM), pl.ds(RIM, RIM)
    to_right = remote(
        nodes.at[pl.ds(rows - RIM, RIM), my_cols], v_late.at[low, my_cols], rim_send.at[0], rim_recv.at[0], right
    )
    to_left = remote(nodes.at[pl.ds(0, RIM), my_cols], v_late.at[high, my_cols], rim_send.at[1], rim_recv.at[1], left)

    @pl.when(has_right)
    def _():
        to_right.start()

    @pl.when(has_left)
    def _():
        to_left.start()

    hub_copies(lambda other: v_hub_src, v_hub, 0)

    for load in loads[5:]:
        load.start()

    ready(v_send_id, v_recv_id)
    ids_s, ids_r = v_send_id[...].reshape(1, count), v_recv_id[...].reshape(1, count)
    col_s = jnp.transpose(jnp.broadcast_to(ids_s, (LANES, count)))[:, 0:1]
    col_r = jnp.transpose(jnp.broadcast_to(ids_r, (LANES, count)))[:, 0:1]
    own_ids = lax.broadcasted_iota(jnp.int32, (1, rows), 1) + me * rows
    late_count = v_late.shape[0]
    late_row = late_ids(lax.broadcasted_iota(jnp.int32, (1, late_count), 1), me, blocks, rows)
    own_col = lax.broadcasted_iota(jnp.int32, (rows, 1), 0) + me * rows
    late_col = late_ids(lax.broadcasted_iota(jnp.int32, (late_count, 1), 0), me, blocks, rows)
    both = lax.broadcasted_iota(jnp.int32, (1, 2 * rows), 1)
    is_recv = both < rows
    both_ids = jnp.where(is_recv, both, both - rows) + me * rows
    oh_own[...] = onehot(jnp.where(is_recv, col_r, col_s), both_ids)
    oh_recv[...] = onehot(col_r, own_ids)
    oh_late[...] = onehot(col_s, late_row)
    t_sums[0:rows, :] = onehot(own_col, ids_r)

    ready(v_nodes, v_recv, v_send)
    terms[0:rows, :] = mm(v_nodes[...], v_recv[...]).astype(BF16)
    terms[rows : 2 * rows, :] = mm(v_nodes[...], v_send[...]).astype(BF16)
    ready(v_edges, v_edge, v_bias)
    for g in groups:
        v_hidden[g, :] = mm(v_edges[g, :], v_edge[...]) + mm(oh_own[g, :], terms[...]) + v_bias[...]

    @pl.when(has_left)
    def _():
        to_right.wait_recv()

    @pl.when(has_right)
    def _():
        to_left.wait_recv()

    rims = pl.ds(0, 2 * RIM)
    rim_swap = remote(v_late.at[rims, my_cols], v_late.at[rims, my_cols], peer_send.at[3], peer_recv.at[3], peer)
    rim_swap.start()
    hub_wait(v_hub, hub_recv.at[0])
    for r in range(HUB_DEV):
        for j in range(pieces):
            part = v_hub[pl.ds(HUB_DEV * j + r, blocks, stride=tile), :]
            h_mine[r * blocks : (r + 1) * blocks, LANES * j : LANES * (j + 1)] = part.astype(BF16)
    hub_swap = remote(h_mine, h_peer, peer_send.at[4], peer_recv.at[4], peer)
    hub_swap.start()
    rim_swap.wait_recv()
    rim_swap.wait_send()
    hub_swap.wait_recv()
    v_late[2 * RIM :, :] = h_mine[...] + h_peer[...]
    late_terms = mm(v_late[...], v_send[...]).astype(BF16)
    for g in groups:
        v_hidden[g, :] += mm(oh_late[g, :], late_terms)
        for at in chunks(g):
            pre = v_hidden[at, :]
            sig = sigmoid(pre)
            act = pre * sig
            v_act[at, :] = act.astype(BF16)
            v_slope[at, :] = sig + act * (1.0 - sig)
    ready(v_out, v_gain_e, v_shift_e)
    for g in groups:
        v_sum[g, :] = mm(v_act[g, :], v_out[...])
        for at in chunks(g):
            total = v_sum[at, :]
            centred = total - mean_row(total)
            inv = lax.rsqrt(mean_row(centred * centred) + epsilon)
            normed = centred * inv
            v_normed[at, :] = normed
            v_scale[at, :] = jnp.broadcast_to(inv, (CHUNK, LANES))
            v_new[at, :] = (v_edges[at, :].astype(F32) + normed * v_gain_e[...] + v_shift_e[...]).astype(BF16)

    g_mine[...] = mm(t_sums[0:rows, :], v_new[...]).astype(BF16)
    gather_copy = remote(g_mine, g_peer, peer_send.at[0], peer_recv.at[0], peer)
    gather_copy.start()

    ready(v_in, v_bias_n, v_mix, v_gain_n, v_shift_n, v_cot)
    v_pre[...] = mm(v_nodes[...], v_in[0:width, :]) + v_bias_n[...]
    t_sums[rows : 2 * rows, :] = onehot(own_col, ids_s)
    t_late[...] = onehot(late_col, ids_s)
    scaled = v_cot[...].astype(F32) * v_gain_n[...]
    v_scaled[...] = scaled - mean_row(scaled)
    gather_copy.wait_recv()
    gathered = (g_mine[...].astype(F32) + g_peer[...].astype(F32)).astype(BF16)
    pre = v_pre[...] + mm(gathered, v_in[width : 2 * width, :])
    sig = sigmoid(pre)
    act = pre * sig
    v_pre[...] = sig + act * (1.0 - sig)
    mix = mm(act.astype(BF16), v_mix[...])
    centred = mix - mean_row(mix)
    inv = lax.rsqrt(mean_row(centred * centred) + epsilon)
    normed = centred * inv
    v_node_normed[...] = normed
    scaled = v_scaled[...]
    dmix = (inv * (scaled - normed * mean_row(scaled * normed))).astype(BF16)
    v_dpre[...] = (mm_t(dmix, v_mix[...]) * v_pre[...]).astype(BF16)
    gathered_grad = mm_t(v_dpre[...], v_in[width : 2 * width, :])
    v_up[...] = gathered_grad.astype(BF16)
    scaled = gathered_grad * v_gain_e[...]
    v_up_scaled[...] = (scaled - mean_row(scaled)).astype(BF16)

    for g in groups:
        v_sum[g, :] = mm(oh_recv[g, :], v_up_scaled[...])
        for at in chunks(g):
            normed = v_normed[at, :]
            scaled = v_sum[at, :]
            v_dsum[at, :] = (v_scale[at, 0:1] * (scaled - normed * mean_row(scaled * normed))).astype(BF16)
    for g in groups:
        v_hidden[g, :] = mm_t(v_dsum[g, :], v_out[...])
        for at in chunks(g):
            v_edpre[at, :] = (v_hidden[at, :] * v_slope[at, :]).astype(BF16)

    late_sums = mm(t_late[...], v_edpre[...]).astype(BF16)
    late_part = mm_t(late_sums, v_send[...])
    e_mine[...] = late_part.astype(BF16)
    late_copy = remote(e_mine, e_peer, peer_send.at[2], peer_recv.at[2], peer)
    late_copy.start()
    sums = mm(t_sums[...], v_edpre[...]).astype(BF16)
    p_mine[...] = (mm_t(sums[0:rows], v_recv[...]) + mm_t(sums[rows : 2 * rows], v_send[...])).astype(BF16)
    part_copy = remote(p_mine, p_peer, peer_send.at[1], peer_recv.at[1], peer)
    part_copy.start()
    late_copy.wait_recv()
    rim_out[...] = (e_mine[0 : 2 * RIM, :].astype(F32) + e_peer[0 : 2 * RIM, :].astype(F32)).astype(BF16)
    back_left = remote(
        rim_out.at[low, my_cols], rim_back.at[high, my_cols], rim_send.at[2], rim_recv.at[2], left
    )
    back_right = remote(
        rim_out.at[high, my_cols], rim_back.at[low, my_cols], rim_send.at[3], rim_recv.at[3], right
    )

    @pl.when(has_left)
    def _():
        back_left.start()

    @pl.when(has_right)
    def _():
        back_right.start()

    hub_part = e_mine[2 * RIM :, :].astype(F32) + e_peer[2 * RIM :, :].astype(F32)
    for r in range(HUB_DEV):
        for j in range(pieces):
            hub_out[pl.ds(HUB_DEV * j + r, blocks, stride=tile), :] = hub_part[
                r * blocks : (r + 1) * blocks, LANES * j : LANES * (j + 1)
            ]

    def hub_tile(other):
        return hub_out.at[pl.ds(pl.multiple_of(other * tile, tile), tile)]

    hub_copies(hub_tile, hub_back, 1)

    for g in groups:
        o_edges[g, :] = (mm(oh_recv[g, :], v_up[...]) + mm_t(v_edpre[g, :], v_edge[...])).astype(BF16)
    o_nodes[...] = (v_nodes[...].astype(F32) + v_node_normed[...] * v_gain_n[...] + v_shift_n[...]).astype(BF16)
    v_direct[...] = v_cot[...].astype(F32) + mm_t(v_dpre[...], v_in[0:width, :])

    part_copy.wait_recv()
    v_direct[...] += p_mine[...].astype(F32) + p_peer[...].astype(F32)

    @pl.when(has_right)
    def _():
        back_left.wait_recv()

    @pl.when(has_left)
    def _():
        back_right.wait_recv()

    back_swap = remote(rim_back.at[:, my_cols], rim_back.at[:, my_cols], peer_send.at[5], peer_recv.at[5], peer)
    back_swap.start()
    hub_wait(hub_back, hub_recv.at[1])
    s_mine[...] = jnp.sum(hub_back[...].reshape(blocks, tile, LANES), axis=0)
    sum_swap = remote(s_mine, s_peer, peer_send.at[6], peer_recv.at[6], peer)
    sum_swap.start()
    o_grad[RIM : rows - RIM, :] = v_direct[RIM : rows - RIM, :].astype(BF16)
    back_swap.wait_recv()
    o_grad[rows - RIM : rows, :] = (v_direct[rows - RIM : rows, :] + rim_back[high, :].astype(F32)).astype(BF16)
    v_direct[0:RIM, :] += rim_back[low, :].astype(F32)
    sum_swap.wait_recv()
    s_peer[...] += s_mine[...]
    for j in range(pieces):
        v_direct[0:HUB_DEV, LANES * j : LANES * (j + 1)] += s_peer[HUB_DEV * j : HUB_DEV * (j + 1), :]
    o_grad[0:RIM, :] = v_direct[0:RIM, :].astype(BF16)

    @pl.when(has_right)
    def _():
        to_right.wait_send()
        back_right.wait_send()

    @pl.when(has_left)
    def _():
        to_left.wait_send()
        back_left.wait_send()

    hub_wait(v_hub, hub_send.at[0])
    hub_wait(hub_out, hub_send.at[1])
    hub_swap.wait_send()
    back_swap.wait_send()
    sum_swap.wait_send()
    gather_copy.wait_send()
    part_copy.wait_send()
    late_copy.wait_send()


def store(*refs):
    sems = refs[-1]
    copies = [pltpu.make_async_copy(refs[k], refs[3 + k], sems.at[k]) for k in range(3)]
    for copy in copies:
        copy.start()
    for copy in copies:
        copy.wait()


def body(
    nodes, edges, senders, receivers, edge_proj, send_proj, recv_proj, edge_bias, edge_out, edge_gain, edge_shift,
    node_in, node_bias, node_out, node_gain, node_shift, node_cot,
):
    blocks = lax.axis_size("space")
    rows, width = nodes.shape
    count = edges.shape[0]
    tile = HUB_DEV * (width // LANES)
    late = 2 * RIM + HUB_DEV * blocks

    def line(vec):
        return vec.reshape(1, -1)

    args = (
        senders, receivers, nodes, edges, edge_proj, send_proj, recv_proj, line(edge_bias), edge_out,
        line(edge_gain), line(edge_shift), node_in, line(node_bias), node_out, line(node_gain), line(node_shift), node_cot,
    )
    any_spec = pl.BlockSpec(memory_space=pl.ANY)
    vmem = pltpu.VMEM
    dma = pltpu.SemaphoreType.DMA
    scratch = [vmem(a.shape, a.dtype) for a in args] + [
        vmem((late, width), BF16),
        vmem((tile, LANES), F32),
        vmem((blocks * tile, LANES), F32),
        vmem((count, 2 * rows), BF16),
        vmem((count, rows), BF16),
        vmem((count, late), BF16),
        vmem((count, width), F32),
        vmem((count, width), F32),
        vmem((count, width), BF16),
        vmem((count, width), F32),
        vmem((count, LANES), F32),
        vmem((count, width), BF16),
        vmem((rows, width), BF16),
        vmem((rows, width), BF16),
        vmem((rows, width), F32),
        vmem((rows, width), BF16),
        vmem((rows, width), F32),
        vmem((rows, width), BF16),
        vmem((count, width), BF16),
        vmem((count, width), BF16),
        vmem((2 * rows, width), BF16),
        vmem((2 * rows, count), BF16),
        vmem((late, count), BF16),
        vmem((count, width), F32),
        vmem((rows, width), F32),
        vmem((rows, width), F32),
        vmem((rows, width), BF16),
        vmem((2 * RIM, width), BF16),
        vmem((2 * RIM, width), BF16),
        vmem((blocks * tile, LANES), F32),
        vmem((blocks * tile, LANES), F32),
        vmem((rows, width), BF16),
        vmem((rows, width), BF16),
        vmem((late, width), BF16),
        vmem((late, width), BF16),
        vmem((16, width), BF16),
        vmem((HUB_DEV * blocks, width), BF16),
        vmem((HUB_DEV * blocks, width), BF16),
        vmem((tile, LANES), F32),
        vmem((tile, LANES), F32),
        dma((len(args),)),
        dma((1,)),
        dma((4,)),
        dma((4,)),
        dma((2,)),
        dma((2,)),
        dma((7,)),
        dma((7,)),
    ]
    results = pl.pallas_call(
        functools.partial(kernel, blocks),
        out_shape=(
            pltpu.VMEM((rows, width), BF16),
            pltpu.VMEM((rows, width), BF16),
            pltpu.VMEM((count, width), BF16),
        ),
        in_specs=[any_spec] * len(args),
        out_specs=(pl.BlockSpec(memory_space=pltpu.VMEM),) * 3,
        scratch_shapes=scratch,
        compiler_params=pltpu.CompilerParams(
            collective_id=0, has_side_effects=True, vmem_limit_bytes=60 * 1024 * 1024
        ),
    )(*args)
    return pl.pallas_call(
        store,
        out_shape=tuple(jax.ShapeDtypeStruct(r.shape, r.dtype) for r in results),
        in_specs=[any_spec] * 3,
        out_specs=(any_spec,) * 3,
        scratch_shapes=[dma((3,))],
        compiler_params=pltpu.CompilerParams(vmem_limit_bytes=2 * 1024 * 1024),
    )(*results)


def solution(mesh):
    in_specs = (
        P("space", None),
        P(("space", "feat"), None),
        P(("space", "feat")),
        P(("space", "feat")),
        *([P()] * 12),
        P("space", None),
    )
    out_specs = (P("space", None), P("space", None), P(("space", "feat"), None))
    return jax.shard_map(body, mesh=mesh, in_specs=in_specs, out_specs=out_specs, check_vma=False)
```

```python
import functools

import jax
import jax.numpy as jnp
from jax import lax
from jax.experimental import pallas as pl
from jax.experimental.pallas import tpu as pltpu
from jax.sharding import PartitionSpec as P

RIM = 48
HUB_DEV = 2
LANES = 128
CHUNK = 32
GROUPS = 2
epsilon = 1e-05

F32 = jnp.float32
BF16 = jnp.bfloat16
MESH = pl.DeviceIdType.MESH


def mm(a, b):
    return jnp.dot(a, b, preferred_element_type=F32)


def mm_t(a, b):
    return lax.dot_general(a, b, (((1,), (1,)), ((), ())), preferred_element_type=F32)


def sigmoid(v):
    return 0.5 * jnp.tanh(0.5 * v) + 0.5


def mean_row(v):
    return jnp.mean(v, axis=-1, keepdims=True)


def late_ids(index, own_block, blocks, rows):
    left = (own_block * rows - RIM) + index
    right = (own_block + 1) * rows + (index - RIM)
    hub = index - 2 * RIM
    row = jnp.zeros_like(hub)
    for step in range(1, HUB_DEV):
        row = row + jnp.where(hub >= step * blocks, 1, 0)
    block = hub - row * blocks
    hub_id = block * rows + row
    hub_id = jnp.where((block == own_block) | (block == own_block + 1), -1, hub_id)
    return jnp.where(index < RIM, left, jnp.where(index < 2 * RIM, right, hub_id))


def onehot(a, b):
    return jnp.where(a == b, 1.0, 0.0).astype(BF16)


def kernel(
    blocks,
    send_id, recv_id, nodes, edges, w_edge, w_send, w_recv, bias, w_out, gain_e, shift_e,
    w_in, bias_n, w_mix, gain_n, shift_n, cot,
    o_nodes, o_grad, o_edges,
    v_send_id, v_recv_id, v_nodes, v_edges, v_edge, v_send, v_recv, v_bias, v_out, v_gain_e, v_shift_e,
    v_in, v_bias_n, v_mix, v_gain_n, v_shift_n, v_cot,
    v_late, v_hub_src, v_hub, oh_own, oh_recv, oh_late,
    v_hidden, v_slope, v_act, v_normed, v_scale, v_new,
    g_mine, g_peer, v_pre, v_dpre, v_direct, v_up, v_dsum, v_edpre,
    terms, t_sums, t_late, v_sum, v_scaled, v_node_normed, v_up_scaled,
    rim_out, rim_back, hub_out, hub_back, p_mine, p_peer, v_head,
    load_sem, head_sem, rim_send, rim_recv, hub_send, hub_recv, peer_send, peer_recv,
):
    me = lax.axis_index("space")
    core = lax.axis_index("feat")
    unroll = blocks - 1 if blocks <= 16 else 5
    rows, width = v_nodes.shape
    count = v_edges.shape[0]
    pieces = width // LANES
    tile = HUB_DEV * pieces
    peer = (me, 1 - core)
    left, right = (me - 1, core), (me + 1, core)
    has_left, has_right = me > 0, me < blocks - 1

    size = count // GROUPS
    groups = [pl.ds(start, size) for start in range(0, count, size)]

    def chunks(g):
        return [pl.ds(start, CHUNK) for start in range(g.start, g.start + size, CHUNK)]

    head_load = pltpu.make_async_copy(nodes.at[pl.ds(0, 16)], v_head, head_sem.at[0])
    head_load.start()
    barrier = pltpu.get_barrier_semaphore()

    def hello(device):
        pl.semaphore_signal(barrier, inc=1, device_id=device, device_id_type=MESH)

    def greet(step, carry):
        hello((lax.rem(me + step, blocks), 0))
        hello((lax.rem(me + step, blocks), 1))
        return carry

    lax.fori_loop(1, blocks, greet, 0, unroll=unroll)
    hello(peer)

    pairs = [
        (nodes, v_nodes), (send_id, v_send_id), (recv_id, v_recv_id), (w_recv, v_recv), (w_send, v_send),
        (edges, v_edges), (w_edge, v_edge), (bias, v_bias), (w_out, v_out), (gain_e, v_gain_e), (shift_e, v_shift_e),
        (w_in, v_in), (bias_n, v_bias_n), (w_mix, v_mix), (gain_n, v_gain_n), (shift_n, v_shift_n), (cot, v_cot),
    ]
    loads = [pltpu.make_async_copy(src, dst, load_sem.at[k]) for k, (src, dst) in enumerate(pairs)]
    for load in loads[:5]:
        load.start()

    def ready(*refs):
        for k, (_, dst) in enumerate(pairs):
            if any(dst is ref for ref in refs):
                loads[k].wait()

    def remote(src, dst, send_sem, recv_sem, device):
        return pltpu.make_async_remote_copy(
            src_ref=src, dst_ref=dst, send_sem=send_sem, recv_sem=recv_sem, device_id=device, device_id_type=MESH
        )

    my_slot = pl.ds(pl.multiple_of(me * tile, tile), tile)

    def hub_copy(step, src, dst, kind):
        other = lax.rem(me + step, blocks)
        return remote(src(other), dst.at[my_slot], hub_send.at[kind], hub_recv.at[kind], (other, core))

    def hub_wait(buffer, sem, times=1):
        part = buffer.at[pl.ds(0, times * (blocks - 1) * tile)]
        pltpu.make_async_copy(part, part, sem).wait()

    head_load.wait()
    head = v_head[...].astype(F32)
    for j in range(pieces):
        v_hub_src[HUB_DEV * j : HUB_DEV * (j + 1), :] = head[0:HUB_DEV, LANES * j : LANES * (j + 1)]
    v_hub[my_slot, :] = v_hub_src[...]
    hub_back[pl.ds(pl.multiple_of(me * 2 * tile, tile), 2 * tile), :] = jnp.zeros((2 * tile, LANES), F32)
    zero_rim = jnp.zeros((RIM, width), BF16)

    @pl.when(jnp.logical_not(has_left))
    def _():
        v_late[0:RIM, :] = zero_rim
        rim_back[0:RIM, :] = zero_rim
        rim_back[2 * RIM : 3 * RIM, :] = zero_rim

    @pl.when(jnp.logical_not(has_right))
    def _():
        v_late[RIM : 2 * RIM, :] = zero_rim
        rim_back[RIM : 2 * RIM, :] = zero_rim
        rim_back[3 * RIM : 4 * RIM, :] = zero_rim

    pl.semaphore_wait(barrier, 2 * blocks - 1)

    low, high = pl.ds(0, RIM), pl.ds(RIM, RIM)
    to_right = remote(nodes.at[pl.ds(rows - RIM, RIM)], v_late.at[low], rim_send.at[0], rim_recv.at[0], right)
    to_left = remote(nodes.at[pl.ds(0, RIM)], v_late.at[high], rim_send.at[1], rim_recv.at[1], left)

    @pl.when(has_right)
    def _():
        to_right.start()

    @pl.when(has_left)
    def _():
        to_left.start()

    def push_hub(step, carry):
        hub_copy(step, lambda other: v_hub_src, v_hub, 0).start()
        return carry

    lax.fori_loop(1, blocks, push_hub, 0, unroll=unroll)

    for load in loads[5:]:
        load.start()

    ready(v_send_id, v_recv_id)
    ids_s, ids_r = v_send_id[...].reshape(1, count), v_recv_id[...].reshape(1, count)
    col_s = jnp.transpose(jnp.broadcast_to(ids_s, (LANES, count)))[:, 0:1]
    col_r = jnp.transpose(jnp.broadcast_to(ids_r, (LANES, count)))[:, 0:1]
    own_ids = lax.broadcasted_iota(jnp.int32, (1, rows), 1) + me * rows
    late_count = v_late.shape[0]
    late_row = late_ids(lax.broadcasted_iota(jnp.int32, (1, late_count), 1), me, blocks, rows)
    own_col = lax.broadcasted_iota(jnp.int32, (rows, 1), 0) + me * rows
    late_col = late_ids(lax.broadcasted_iota(jnp.int32, (late_count, 1), 0), me, blocks, rows)
    both = lax.broadcasted_iota(jnp.int32, (1, 2 * rows), 1)
    is_recv = both < rows
    both_ids = jnp.where(is_recv, both, both - rows) + me * rows
    oh_own[...] = onehot(jnp.where(is_recv, col_r, col_s), both_ids)
    oh_recv[...] = onehot(col_r, own_ids)
    oh_late[...] = onehot(col_s, late_row)
    t_sums[0:rows, :] = onehot(own_col, ids_r)

    ready(v_nodes, v_recv, v_send)
    terms[0:rows, :] = mm(v_nodes[...], v_recv[...]).astype(BF16)
    terms[rows : 2 * rows, :] = mm(v_nodes[...], v_send[...]).astype(BF16)
    ready(v_edges, v_edge, v_bias)
    for g in groups:
        v_hidden[g, :] = mm(v_edges[g, :], v_edge[...]) + mm(oh_own[g, :], terms[...]) + v_bias[...]

    @pl.when(has_left)
    def _():
        to_right.wait_recv()

    @pl.when(has_right)
    def _():
        to_left.wait_recv()

    hub_wait(v_hub, hub_recv.at[0])
    for r in range(HUB_DEV):
        for j in range(pieces):
            part = v_hub[pl.ds(HUB_DEV * j + r, blocks, stride=tile), :]
            v_late[2 * RIM + r * blocks : 2 * RIM + (r + 1) * blocks, LANES * j : LANES * (j + 1)] = part.astype(BF16)
    late_terms = mm(v_late[...], v_send[...]).astype(BF16)
    for g in groups:
        v_hidden[g, :] += mm(oh_late[g, :], late_terms)
        for at in chunks(g):
            pre = v_hidden[at, :]
            sig = sigmoid(pre)
            act = pre * sig
            v_act[at, :] = act.astype(BF16)
            v_slope[at, :] = sig + act * (1.0 - sig)
    ready(v_out, v_gain_e, v_shift_e)
    for g in groups:
        v_sum[g, :] = mm(v_act[g, :], v_out[...])
        for at in chunks(g):
            total = v_sum[at, :]
            centred = total - mean_row(total)
            inv = lax.rsqrt(mean_row(centred * centred) + epsilon)
            normed = centred * inv
            v_normed[at, :] = normed
            v_scale[at, :] = jnp.broadcast_to(inv, (CHUNK, LANES))
            v_new[at, :] = (v_edges[at, :].astype(F32) + normed * v_gain_e[...] + v_shift_e[...]).astype(BF16)

    g_mine[...] = mm(t_sums[0:rows, :], v_new[...]).astype(BF16)
    gather_copy = remote(g_mine, g_peer, peer_send.at[0], peer_recv.at[0], peer)
    gather_copy.start()

    ready(v_in, v_bias_n, v_mix, v_gain_n, v_shift_n, v_cot)
    v_pre[...] = mm(v_nodes[...], v_in[0:width, :]) + v_bias_n[...]
    t_sums[rows : 2 * rows, :] = onehot(own_col, ids_s)
    t_late[...] = onehot(late_col, ids_s)
    scaled = v_cot[...].astype(F32) * v_gain_n[...]
    v_scaled[...] = scaled - mean_row(scaled)
    gather_copy.wait_recv()
    gathered = (g_mine[...].astype(F32) + g_peer[...].astype(F32)).astype(BF16)
    pre = v_pre[...] + mm(gathered, v_in[width : 2 * width, :])
    sig = sigmoid(pre)
    act = pre * sig
    v_pre[...] = sig + act * (1.0 - sig)
    mix = mm(act.astype(BF16), v_mix[...])
    centred = mix - mean_row(mix)
    inv = lax.rsqrt(mean_row(centred * centred) + epsilon)
    normed = centred * inv
    v_node_normed[...] = normed
    scaled = v_scaled[...]
    dmix = (inv * (scaled - normed * mean_row(scaled * normed))).astype(BF16)
    v_dpre[...] = (mm_t(dmix, v_mix[...]) * v_pre[...]).astype(BF16)
    gathered_grad = mm_t(v_dpre[...], v_in[width : 2 * width, :])
    v_up[...] = gathered_grad.astype(BF16)
    scaled = gathered_grad * v_gain_e[...]
    v_up_scaled[...] = (scaled - mean_row(scaled)).astype(BF16)

    for g in groups:
        v_sum[g, :] = mm(oh_recv[g, :], v_up_scaled[...])
        for at in chunks(g):
            normed = v_normed[at, :]
            scaled = v_sum[at, :]
            v_dsum[at, :] = (v_scale[at, 0:1] * (scaled - normed * mean_row(scaled * normed))).astype(BF16)
    for g in groups:
        v_hidden[g, :] = mm_t(v_dsum[g, :], v_out[...])
        for at in chunks(g):
            v_edpre[at, :] = (v_hidden[at, :] * v_slope[at, :]).astype(BF16)

    late_sums = mm(t_late[...], v_edpre[...]).astype(BF16)
    late_part = mm_t(late_sums, v_send[...])
    rim_out[...] = late_part[0 : 2 * RIM, :].astype(BF16)

    def back(src, side, first, device, k):
        place = pl.ds(pl.multiple_of((2 * core + side) * RIM, 16), RIM)
        return remote(rim_out.at[src], rim_back.at[place], rim_send.at[first + k], rim_recv.at[first + core], device)

    back_left = [back(low, 1, 2, (me - 1, k), k) for k in range(2)]
    back_right = [back(high, 0, 4, (me + 1, k), k) for k in range(2)]

    @pl.when(has_left)
    def _():
        for copy in back_left:
            copy.start()

    @pl.when(has_right)
    def _():
        for copy in back_right:
            copy.start()

    hub_part = late_part[2 * RIM :, :]
    for r in range(HUB_DEV):
        for j in range(pieces):
            hub_out[pl.ds(HUB_DEV * j + r, blocks, stride=tile), :] = hub_part[
                r * blocks : (r + 1) * blocks, LANES * j : LANES * (j + 1)
            ]

    def hub_tile(other):
        return hub_out.at[pl.ds(pl.multiple_of(other * tile, tile), tile)]

    slot = pl.ds(pl.multiple_of((2 * me + core) * tile, tile), tile)

    def return_hub(step, carry):
        other = lax.rem(me + step, blocks)
        for k in range(2):
            remote(hub_tile(other), hub_back.at[slot], hub_send.at[1], hub_recv.at[1], (other, k)).start()
        return carry

    lax.fori_loop(1, blocks, return_hub, 0, unroll=unroll)

    sums = mm(t_sums[...], v_edpre[...]).astype(BF16)
    p_mine[...] = (mm_t(sums[0:rows], v_recv[...]) + mm_t(sums[rows : 2 * rows], v_send[...])).astype(BF16)
    part_copy = remote(p_mine, p_peer, peer_send.at[1], peer_recv.at[1], peer)
    part_copy.start()

    for g in groups:
        o_edges[g, :] = (mm(oh_recv[g, :], v_up[...]) + mm_t(v_edpre[g, :], v_edge[...])).astype(BF16)
    o_nodes[...] = (v_nodes[...].astype(F32) + v_node_normed[...] * v_gain_n[...] + v_shift_n[...]).astype(BF16)
    v_direct[...] = v_cot[...].astype(F32) + mm_t(v_dpre[...], v_in[0:width, :])

    part_copy.wait_recv()
    v_direct[...] += p_mine[...].astype(F32) + p_peer[...].astype(F32)

    def landed(side, first):
        for k in range(2):
            part = rim_back.at[pl.ds((2 * k + side) * RIM, RIM)]
            remote(part, part, rim_send.at[first + k], rim_recv.at[first + k], peer).wait_recv()

    @pl.when(has_right)
    def _():
        landed(1, 2)

    @pl.when(has_left)
    def _():
        landed(0, 4)

    rim_sum = rim_back[0 : 2 * RIM, :].astype(F32) + rim_back[2 * RIM : 4 * RIM, :].astype(F32)
    o_grad[RIM : rows - RIM, :] = v_direct[RIM : rows - RIM, :].astype(BF16)
    o_grad[rows - RIM : rows, :] = (v_direct[rows - RIM : rows, :] + rim_sum[RIM : 2 * RIM]).astype(BF16)
    v_direct[0:RIM, :] += rim_sum[0:RIM]
    hub_wait(hub_back, hub_recv.at[1], 2)
    hub_wait(v_hub, hub_send.at[0])
    v_hub_src[...] = jnp.sum(hub_back[...].reshape(2 * blocks, tile, LANES), axis=0)
    for j in range(pieces):
        v_direct[0:HUB_DEV, LANES * j : LANES * (j + 1)] += v_hub_src[HUB_DEV * j : HUB_DEV * (j + 1), :]
    o_grad[0:RIM, :] = v_direct[0:RIM, :].astype(BF16)

    @pl.when(has_right)
    def _():
        to_right.wait_send()
        for copy in back_right:
            copy.wait_send()

    @pl.when(has_left)
    def _():
        to_left.wait_send()
        for copy in back_left:
            copy.wait_send()

    hub_wait(hub_back, hub_send.at[1], 2)
    gather_copy.wait_send()
    part_copy.wait_send()


def store(*refs):
    sems = refs[-1]
    copies = [pltpu.make_async_copy(refs[k], refs[3 + k], sems.at[k]) for k in range(3)]
    for copy in copies:
        copy.start()
    for copy in copies:
        copy.wait()


def body(
    nodes, edges, senders, receivers, edge_proj, send_proj, recv_proj, edge_bias, edge_out, edge_gain, edge_shift,
    node_in, node_bias, node_out, node_gain, node_shift, node_cot,
):
    blocks = lax.axis_size("space")
    rows, width = nodes.shape
    count = edges.shape[0]
    tile = HUB_DEV * (width // LANES)
    late = 2 * RIM + HUB_DEV * blocks

    def line(vec):
        return vec.reshape(1, -1)

    args = (
        senders, receivers, nodes, edges, edge_proj, send_proj, recv_proj, line(edge_bias), edge_out,
        line(edge_gain), line(edge_shift), node_in, line(node_bias), node_out, line(node_gain), line(node_shift), node_cot,
    )
    any_spec = pl.BlockSpec(memory_space=pl.ANY)
    vmem = pltpu.VMEM
    dma = pltpu.SemaphoreType.DMA
    scratch = [vmem(a.shape, a.dtype) for a in args] + [
        vmem((late, width), BF16),
        vmem((tile, LANES), F32),
        vmem((blocks * tile, LANES), F32),
        vmem((count, 2 * rows), BF16),
        vmem((count, rows), BF16),
        vmem((count, late), BF16),
        vmem((count, width), F32),
        vmem((count, width), F32),
        vmem((count, width), BF16),
        vmem((count, width), F32),
        vmem((count, LANES), F32),
        vmem((count, width), BF16),
        vmem((rows, width), BF16),
        vmem((rows, width), BF16),
        vmem((rows, width), F32),
        vmem((rows, width), BF16),
        vmem((rows, width), F32),
        vmem((rows, width), BF16),
        vmem((count, width), BF16),
        vmem((count, width), BF16),
        vmem((2 * rows, width), BF16),
        vmem((2 * rows, count), BF16),
        vmem((late, count), BF16),
        vmem((count, width), F32),
        vmem((rows, width), F32),
        vmem((rows, width), F32),
        vmem((rows, width), BF16),
        vmem((2 * RIM, width), BF16),
        vmem((4 * RIM, width), BF16),
        vmem((blocks * tile, LANES), F32),
        vmem((2 * blocks * tile, LANES), F32),
        vmem((rows, width), BF16),
        vmem((rows, width), BF16),
        vmem((16, width), BF16),
        dma((len(args),)),
        dma((1,)),
        dma((6,)),
        dma((6,)),
        dma((2,)),
        dma((2,)),
        dma((3,)),
        dma((3,)),
    ]
    results = pl.pallas_call(
        functools.partial(kernel, blocks),
        out_shape=(
            pltpu.VMEM((rows, width), BF16),
            pltpu.VMEM((rows, width), BF16),
            pltpu.VMEM((count, width), BF16),
        ),
        in_specs=[any_spec] * len(args),
        out_specs=(pl.BlockSpec(memory_space=pltpu.VMEM),) * 3,
        scratch_shapes=scratch,
        compiler_params=pltpu.CompilerParams(
            collective_id=0, has_side_effects=True, vmem_limit_bytes=60 * 1024 * 1024
        ),
    )(*args)
    return pl.pallas_call(
        store,
        out_shape=tuple(jax.ShapeDtypeStruct(r.shape, r.dtype) for r in results),
        in_specs=[any_spec] * 3,
        out_specs=(any_spec,) * 3,
        scratch_shapes=[dma((3,))],
        compiler_params=pltpu.CompilerParams(vmem_limit_bytes=2 * 1024 * 1024),
    )(*results)


def solution(mesh):
    in_specs = (
        P("space", None),
        P(("space", "feat"), None),
        P(("space", "feat")),
        P(("space", "feat")),
        *([P()] * 12),
        P("space", None),
    )
    out_specs = (P("space", None), P("space", None), P(("space", "feat"), None))
    return jax.shard_map(body, mesh=mesh, in_specs=in_specs, out_specs=out_specs, check_vma=False)
```
